256 devices in a mesh: group: 8 (over y, z_hi), ctx: 32 (over x, z_lo, core).
Axes of the slice: x: 4, y: 4, z: 8 (z_hi: 2, z_lo: 4; z = z_hi * 4 + z_lo), core: 2. Of those that a mesh axis runs over, the one named last changes fastest.
Arguments:
- queries: bfloat16 [2048, 5120], P(('group', 'ctx')), may hold values from -10 to 10
- grad_out: bfloat16 [2048, 5120], P(('group', 'ctx')), may hold values from -6 to 6
- keys: bfloat16 [16384, 1024], P('ctx'), may hold values from -6 to 6
- values: bfloat16 [16384, 1024], P('ctx'), may hold values from -6 to 6
- prompt_len: int32 [1], replicated, may hold values from 16128 to 16384
- resp_len: int32 [8, 2], P('group'), may hold values from 64 to 128
Outputs:
- query_grad: bfloat16 [2048, 5120], P(('group', 'ctx'))
- key_grad: bfloat16 [16384, 1024], P('ctx', 'group')
- value_grad: bfloat16 [16384, 1024], P('ctx', 'group')
The draws below stay inside these ranges and needn't reach their ends.
All inputs are finite; a program needn't handle non-finite values.
Results may differ from the reference program's by a relative error of at most 0.018.
Values may be sent and summed in bfloat16 or wider, within the bound.
A program may use at most 64 MiB of HBM per device.

```python
import jax
import jax.numpy as jnp
from jax import lax

QH = 40
KH = 8
HD = 128
RESP = 2
WINDOW = 128
PD = 512
GROUPS = 8
ROWS = 256
PROMPT = 16384


def paired_draw(key, blend, low_scale, high_scale):
    key_keys = jax.random.fold_in(key, 101)
    key_query = jax.random.fold_in(key, 102)
    key_select = jax.random.fold_in(key, 106)
    npair = min(64, PROMPT // 2 - PD // 2)
    half = PROMPT // 2
    place = jnp.arange(PROMPT, dtype=jnp.float32) / (PROMPT - 1)
    ramp = low_scale * jnp.exp(place * jnp.log(high_scale / low_scale))
    base_keys = jnp.clip(jax.random.normal(key_keys, (PROMPT, KH * HD), jnp.float32) * ramp[:, None], -6.0, 6.0)
    firsts_rows = base_keys[:npair]
    mixed_rows = base_keys[half:half + npair]
    new_keys = base_keys.at[:npair].set(firsts_rows).at[half:half + npair].set(mixed_rows)
    count = GROUPS * ROWS
    base_query = jnp.clip(jax.random.normal(key_query, (count, QH, HD), jnp.float32), -6.0, 6.0)
    chosen = (jax.random.randint(key_select, (count, QH), 0, 40) == 0).astype(jnp.float32) * blend
    query_all = base_query * (1.0 - chosen[..., None])
    return (query_all.reshape(count, QH * HD), new_keys)


def draw_queries(key, part):
    query_all, new_keys = paired_draw(key, 0.0, 0.6, 1.8)
    return query_all.astype(jnp.bfloat16)


def draw_keys(key, part):
    query_all, new_keys = paired_draw(key, 0.0, 0.6, 1.8)
    return new_keys.astype(jnp.bfloat16)


def set_ends(entries, rng, smallest, largest):
    dims = entries.shape
    spot = [jax.random.randint(jax.random.fold_in(rng, axis), (), 0, dims[axis]) for axis in range(len(dims))]
    entries = entries.at[tuple(spot)].set(smallest)
    longest = dims.index(max(dims))
    spot[longest] = (spot[longest] + 1) % dims[longest]
    return entries.at[tuple(spot)].set(largest)


def level_of(own_key, extent, pieces, least, largest):
    factor_of = 1.0
    for axis_at, shards_of in pieces:
        heights = jax.random.uniform(jax.random.fold_in(jax.random.fold_in(own_key, 6), axis_at), (shards_of,), jnp.float32, least / len(pieces), largest / len(pieces))
        factor_of = factor_of * jnp.repeat(jnp.exp(heights), extent[axis_at] // shards_of).reshape((-1,) + (1,) * (len(extent) - 1 - axis_at))
    return factor_of


def scatter_about(own_key, dims, width, bound, shards=(), held_as=jnp.bfloat16):
    array = jax.random.normal(own_key, dims, jnp.float32) * width
    if len(shards) > 0:
        array = level_of(own_key, dims, shards, -0.22, 0.18) * array
    return jnp.clip(array, min=-bound, max=bound).astype(held_as)


def setup_inputs(seed: int = 0) -> dict:
    seeds = jax.random.split(jax.random.key(seed), 7)
    queries = draw_queries(jax.random.fold_in(seeds[6], 71), 0)
    grad_out = scatter_about(seeds[1], (GROUPS * ROWS, QH * HD), 1.0, 6.0, ((0, 256),))
    keys = draw_keys(jax.random.fold_in(seeds[6], 71), 0)
    values = scatter_about(seeds[3], (PROMPT, KH * HD), 1.0, 6.0, ((0, 32),))
    prompt_len = jax.random.randint(seeds[4], (1,), PROMPT - PD // 2, PROMPT + 1).astype(jnp.int32)
    resp_len = set_ends(jax.random.randint(seeds[5], (GROUPS, RESP), WINDOW // 2, WINDOW + 1), jax.random.fold_in(seeds[5], 1), WINDOW // 2, WINDOW).astype(jnp.int32)
    return dict(queries=queries, grad_out=grad_out, keys=keys, values=values, prompt_len=prompt_len, resp_len=resp_len)


def reference(queries, grad_out, keys, values, prompt_len, resp_len):
    share = QH // KH
    scale = 1.0 / (HD ** 0.5)
    key_ok = jnp.arange(PROMPT, dtype=jnp.int32) < prompt_len[0]
    rows = jnp.arange(ROWS, dtype=jnp.int32)
    which = rows // WINDOW
    picks = jnp.arange(RESP, dtype=jnp.int32)

    def per_group(carry, inputs):
        q_group, do_group, len_group = inputs
        limit = jnp.sum(jnp.where(which[:, None] == picks[None, :], len_group[None, :], 0), axis=1)
        live = (rows % WINDOW) < limit
        masked = jnp.where(live[:, None], do_group, jnp.zeros_like(do_group))

        def per_head(head):
            q_head = lax.dynamic_slice_in_dim(q_group, head * share * HD, share * HD, 1).reshape(ROWS, share, HD).astype(jnp.float32)
            do_head = lax.dynamic_slice_in_dim(masked, head * share * HD, share * HD, 1).reshape(ROWS, share, HD).astype(jnp.float32)
            k_head = lax.dynamic_slice_in_dim(keys, head * HD, HD, 1).astype(jnp.float32)
            v_head = lax.dynamic_slice_in_dim(values, head * HD, HD, 1).astype(jnp.float32)
            scores = jnp.einsum('rgd,kd->grk', q_head, k_head) * scale
            scores = jnp.where(key_ok[None, None, :], scores, jnp.float32(-1e30))
            top = jnp.max(scores, axis=-1, keepdims=True)
            expo = jnp.exp(scores - top)
            probs = expo / jnp.sum(expo, axis=-1, keepdims=True)
            dprobs = jnp.einsum('rgd,kd->grk', do_head, v_head)
            row_dot = jnp.sum(probs * dprobs, axis=-1, keepdims=True)
            dscores = (probs * (dprobs - row_dot) * scale).astype(jnp.bfloat16).astype(jnp.float32)
            probs_low = probs.astype(jnp.bfloat16).astype(jnp.float32)
            dq = jnp.einsum('grk,kd->rgd', dscores, k_head).reshape(ROWS, share * HD)
            dk = jnp.einsum('grk,rgd->kd', dscores, q_head)
            dv = jnp.einsum('grk,rgd->kd', probs_low, do_head)
            return dq, dk, dv

        dq, dk, dv = lax.map(per_head, jnp.arange(KH, dtype=jnp.int32))
        dq = jnp.transpose(dq, (1, 0, 2)).reshape(ROWS, QH * HD).astype(jnp.bfloat16)
        dk = jnp.transpose(dk, (1, 0, 2)).reshape(PROMPT, KH * HD)
        dv = jnp.transpose(dv, (1, 0, 2)).reshape(PROMPT, KH * HD)
        return (carry[0] + dk, carry[1] + dv), dq

    start = (jnp.zeros((PROMPT, KH * HD), jnp.float32), jnp.zeros((PROMPT, KH * HD), jnp.float32))
    inputs = (queries.reshape(GROUPS, ROWS, QH * HD), grad_out.reshape(GROUPS, ROWS, QH * HD), resp_len)
    totals, dq_all = lax.scan(per_group, start, inputs)
    query_grad = dq_all.reshape(GROUPS * ROWS, QH * HD)
    return query_grad, totals[0].astype(jnp.bfloat16), totals[1].astype(jnp.bfloat16)
```

```python
import functools
import math

import jax
import jax.numpy as jnp
from jax import lax
from jax.experimental import pallas as pl
from jax.experimental.pallas import tpu as pltpu
from jax.sharding import PartitionSpec as P

QH = 40
KH = 8
HD = 128
SHARE = QH // KH
WINDOW = 128
SPAN = 512
OWN = 8
BLK = OWN * SHARE
UNIT = 16 * BLK
KT = 256
KEYS = 4 * SPAN
NT = KEYS // KT
SCALE = 1.0 / math.sqrt(HD)
LOG2 = SCALE * math.log2(math.e)
TRANS = (((1,), (1,)), ((), ()))
MESH = pl.DeviceIdType.MESH
F32 = jnp.float32
BF16 = jnp.bfloat16


def dot(a, b):
    return jnp.dot(a, b, preferred_element_type=F32)


def dot_t(a, b):
    return lax.dot_general(a, b, TRANS, preferred_element_type=F32)


def wide(rows):
    return jnp.concatenate([rows[i : i + 1] for i in range(SHARE)], axis=1)


def tall(row):
    return jnp.concatenate([row[:, i * HD : (i + 1) * HD] for i in range(SHARE)], axis=0)


def kernel(
    plen_ref, rlen_ref, q_ref, do_ref, k_hbm, v_hbm,
    dq_ref, dk_ref, dv_ref,
    snd, gath, q_s, do_s, kv, k_t, e_buf, dp_buf, mst, st_all, dka, dva,
    dq_own, dq_out, dq_in, z_out, z_in, f_out, f_in, c_out, c_in, zz_out, zz_in,
    loc_sem, kv_send, kv_recv, s1_send, s1_recv, x_send, x_recv, st_send, st_recv,
    dq_send, dq_recv, z_sem, f_send, f_recv, c_sem, zz_sem,
):
    g = lax.axis_index("group")
    c = lax.axis_index("ctx")
    core = c % 2
    z_lo = (c // 2) % 4
    x = c // 8
    par = z_lo % 2
    zl = z_lo // 2
    me16 = zl * 8 + g
    me8 = x * 2 + zl
    other = 1 - zl

    def ctx_of(x_, z_lo_, core_):
        return (x_ * 4 + z_lo_) * 2 + core_

    sib = (g, ctx_of(x, z_lo, 1 - core))
    zp_lo = z_lo + 1 - 2 * par
    zp = (g, ctx_of(x, zp_lo, core))
    mate = (g, ctx_of(x, other * 2 + par, core))

    def plane(k):
        dest = (me16 + k) % 16
        return (dest % 8, ctx_of(x, (dest // 8) * 2 + par, core))

    def ring(k):
        dest = (me8 + k) % 8
        return (g, ctx_of(dest // 2, (dest % 2) * 2 + par, core))

    def at_x(k):
        return (g, ctx_of((x + k) % 4, z_lo, core))

    def remote(src, dst, send, recv, dev):
        return pltpu.make_async_remote_copy(
            src_ref=src, dst_ref=dst, send_sem=send, recv_sem=recv, device_id=dev, device_id_type=MESH
        )

    barrier = pltpu.get_barrier_semaphore()

    def greet(dev):
        pl.semaphore_signal(barrier, inc=1, device_id=dev, device_id_type=MESH)

    lax.fori_loop(1, 16, lambda k, s: (greet(plane(k)), s)[1], 0)
    for dx in (1, 2, 3):
        for z_ in (zl, other):
            greet((g, ctx_of((x + dx) % 4, z_ * 2 + par, core)))
    greet(sib)
    greet(zp)

    cols = pl.ds(pl.multiple_of(g * HD, HD), HD)
    local = [
        pltpu.make_async_copy(h.at[:, cols], kv.at[0, i], loc_sem.at[i]) for i, h in enumerate((k_hbm, v_hbm))
    ]
    for cp in local:
        cp.start()

    qf = q_ref[...].astype(F32)
    live_to = rlen_ref[0, c // 16]
    t_row = (c % 16) * OWN + lax.broadcasted_iota(jnp.int32, (OWN, 1), 0)
    dof = jnp.where(t_row < live_to, do_ref[...].astype(F32), 0.0)
    for b in range(KH):
        rows = [m[:, (b * SHARE + a) * HD : (b * SHARE + a + 1) * HD] for m in (qf, dof) for a in range(SHARE)]
        snd[b] = jnp.concatenate(rows, axis=0).astype(BF16)
    gath[x, me16] = snd[g]

    pl.semaphore_wait(barrier, 23)

    def s1(k):
        return remote(snd.at[plane(k)[0]], gath.at[x, me16], s1_send.at[k], s1_recv.at[me16], plane(k))

    def s1_start(k, s):
        s1(k).start()
        return s

    lax.fori_loop(1, 16, s1_start, 0)

    def kv_copy(i, src, slot, dev):
        return remote(src, kv.at[slot, i], kv_send.at[slot, i], kv_recv.at[slot, i], dev)

    for i, h in enumerate((k_hbm, v_hbm)):
        kv_copy(i, h.at[:, cols], 2, zp).start()
        kv_copy(i, h.at[:, cols], 1, sib).start()

    dka[...] = jnp.zeros_like(dka)
    dva[...] = jnp.zeros_like(dva)

    plen = plen_ref[0]
    c_slots = [c, sib[1], zp[1], ctx_of(x, zp_lo, 1 - core)]

    def piece(x_, p):
        return gath.at[x_, pl.ds(p * 4, 4)]

    def x_copy(way, p):
        if way == 0:
            return remote(piece(x, p), piece(x, p), x_send.at[0, p], x_recv.at[0, p], at_x(1))
        if way == 1:
            return remote(piece(x, p), piece(x, p), x_send.at[1, p], x_recv.at[1, p], at_x(3))
        src = (x + 3) % 4 if p < 2 else (x + 1) % 4
        return remote(piece(src, p), piece(src, p), x_send.at[2, p], x_recv.at[2, p], at_x(1 if p < 2 else 3))

    def s1_wait(k, s):
        src = (me16 + k) % 16
        remote(snd.at[0], gath.at[x, src], s1_send.at[k], s1_recv.at[src], plane(k)).wait_recv()
        return s

    def st_copy(unit, k):
        return remote(
            st_all.at[unit, me8], st_all.at[unit, me8], st_send.at[unit, k], st_recv.at[unit, me8], ring(k)
        )

    def phase1(i, carry):
        unit = (x + i + i // 2 - 2 * (i // 3)) % 4

        @pl.when(i == 0)
        def _():
            lax.fori_loop(1, 16, s1_wait, 0)
            for p, r in ((0, 2), (1, 3), (2, 0), (3, 1)):
                x_copy(0, p).start()
                x_copy(1, r).start()
            for i_ in range(2):
                kv_copy(i_, kv.at[2, i_], 2, zp).wait_recv()
                kv_copy(i_, kv.at[2, i_], 3, sib).start()
            for cp in local:
                cp.wait()
            for i_ in range(2):
                kv_copy(i_, kv.at[1, i_], 1, sib).wait_recv()
            for i_ in range(2):
                kv_copy(i_, kv.at[3, i_], 3, sib).wait_recv()
            for slot in range(4):
                k_t[:, slot * SPAN : (slot + 1) * SPAN] = kv[slot, 0].astype(F32).T.astype(BF16)

        @pl.when(i == 1)
        def _():
            for p, r in ((0, 2), (1, 3)):
                x_copy(0, p).wait_recv()
                x_copy(2, p).start()
                x_copy(1, r).wait_recv()
                x_copy(2, r).start()
            for r in (0, 1):
                x_copy(1, r).wait_recv()

        @pl.when(i == 2)
        def _():
            for p in (2, 3):
                x_copy(0, p).wait_recv()

        @pl.when(i == 3)
        def _():
            for p in range(4):
                x_copy(2, p).wait_recv()

        both = gath[unit].astype(F32)
        qu = both[:, :BLK].reshape(UNIT, HD).astype(BF16)
        dou = both[:, BLK:].reshape(UNIT, HD).astype(BF16)
        q_s[unit] = qu
        do_s[unit] = dou
        tops, sums, dots = [], [], []
        for t in range(NT):
            slot, part = t * KT // SPAN, pl.ds(t * KT % SPAN, KT)
            rows = pl.ds(t * KT, KT)
            s = dot_t(kv[slot, 0, part], qu)
            if t % 2 == 1:
                place = c_slots[slot] * SPAN + KT + lax.broadcasted_iota(jnp.int32, (KT, 1), 0)
                s = jnp.where(place < plen, s, -1e30)
            dp = dot_t(kv[slot, 1, part], dou)
            top = jnp.max(s, axis=0, keepdims=True)
            e = jnp.exp2((s - top) * LOG2)
            e_buf[unit, rows] = e
            dp_buf[unit, rows] = dp
            tops.append(top)
            sums.append(jnp.sum(e, axis=0, keepdims=True))
            dots.append(jnp.sum(e * dp, axis=0, keepdims=True))
        top = functools.reduce(jnp.maximum, tops)
        total, rdot = 0.0, 0.0
        for t in range(NT):
            w = jnp.exp2((tops[t] - top) * LOG2)
            total = total + sums[t] * w
            rdot = rdot + dots[t] * w
        mst[unit] = jnp.concatenate(tops, axis=0)
        st_all[unit, me8] = jnp.concatenate([tall(top), tall(total), tall(rdot), jnp.zeros((1, HD), F32)], axis=0)

        def send(k, s):
            st_copy(unit, k).start()
            return s

        lax.fori_loop(1, 8, send, 0)
        return carry

    lax.fori_loop(0, 4, phase1, 0)

    def dq_copy(unit):
        return remote(dq_out.at[unit], dq_in.at[x], dq_send.at[unit], dq_recv.at[x], (g, ctx_of(unit, z_lo, core)))

    def phase2(i, carry):
        unit = (x + i) % 4

        def arrived(k, s):
            src = (me8 + k) % 8
            remote(
                st_all.at[unit, src], st_all.at[unit, src], st_send.at[unit, k], st_recv.at[unit, src], ring(k)
            ).wait_recv()
            return s

        lax.fori_loop(1, 8, arrived, 0)
        stats = st_all[unit]
        top = jnp.max(stats[:, 0:SHARE], axis=0)
        w = jnp.exp2((stats[:, 0:SHARE] - top[None]) * LOG2)
        total = jnp.sum(stats[:, SHARE : 2 * SHARE] * w, axis=0)
        rdot = jnp.sum(stats[:, 2 * SHARE : 3 * SHARE] * w, axis=0) / total
        top, inv, rdot = wide(top), wide(1.0 / total), wide(rdot)
        qu, dou = q_s[unit], do_s[unit]
        factor = jnp.exp2((mst[unit] - top) * LOG2) * inv
        dq_t = jnp.zeros((HD, UNIT), F32)
        for t in range(NT):
            rows = pl.ds(t * KT, KT)
            p = e_buf[unit, rows] * factor[t : t + 1]
            ds = (p * (dp_buf[unit, rows] - rdot)).astype(BF16)
            dva[rows] += dot(p.astype(BF16), dou)
            dka[rows] += dot(ds, qu)
            dq_t += dot(k_t[:, rows], ds)
        dq = dq_t.T * SCALE

        @pl.when(i < 4)
        def _():
            dq_out[unit] = dq.astype(BF16)
            dq_copy(unit).start()

        @pl.when(i == 4)
        def _():
            dq_own[...] = dq

        return carry

    lax.fori_loop(1, 5, phase2, 0)

    for n, slot in enumerate((1, 3)):
        rows = pl.ds(slot * SPAN, SPAN)
        c_out[n, 0] = (dka[rows] * SCALE).astype(BF16)
        c_out[n, 1] = dva[rows].astype(BF16)
    c_copy = remote(c_out, c_in, c_sem.at[0], c_sem.at[1], sib)
    c_copy.start()

    tot = dq_own[...]
    for k in (1, 2, 3):
        src = (x + k) % 4
        remote(dq_out.at[src], dq_in.at[src], dq_send.at[src], dq_recv.at[src], at_x(k)).wait_recv()
        tot = tot + dq_in[src].astype(F32)
    dq_own[...] = tot
    z_out[...] = dq_own[pl.ds(pl.multiple_of(other * 320, 320), 320)].astype(BF16)
    z_copy = remote(z_out, z_in, z_sem.at[0], z_sem.at[1], mate)
    z_copy.start()

    c_copy.wait_recv()
    far = pl.ds(2 * SPAN, SPAN)
    zz_out[0] = (dka[far] * SCALE + c_in[1, 0].astype(F32)).astype(BF16)
    zz_out[1] = (dva[far] + c_in[1, 1].astype(F32)).astype(BF16)
    zz_copy = remote(zz_out, zz_in, zz_sem.at[0], zz_sem.at[1], zp)
    zz_copy.start()

    z_copy.wait_recv()
    mine = dq_own[pl.ds(pl.multiple_of(zl * 320, 320), 320)] + z_in[...].astype(F32)
    for b in range(8):
        f_out[b] = jnp.concatenate([mine[b * BLK : (b + 1) * BLK], jnp.zeros((8, HD), F32)], axis=0).astype(BF16)
    f_in[g] = f_out[g]

    def f_copy(k):
        dest = (g + k) % 8
        return remote(f_out.at[dest], f_in.at[g], f_send.at[k], f_recv.at[g], (dest, c))

    def f_start(k, s):
        f_copy(k).start()
        return s

    lax.fori_loop(1, 8, f_start, 0)

    zz_copy.wait_recv()
    near = pl.ds(0, SPAN)
    dk_ref[...] = (dka[near] * SCALE + c_in[0, 0].astype(F32) + zz_in[0].astype(F32)).astype(BF16)
    dv_ref[...] = (dva[near] + c_in[0, 1].astype(F32) + zz_in[1].astype(F32)).astype(BF16)

    def f_wait(k, s):
        src = (g + k) % 8
        remote(f_out.at[src], f_in.at[src], f_send.at[k], f_recv.at[src], (src, c)).wait_recv()
        return s

    lax.fori_loop(1, 8, f_wait, 0)
    out = []
    for b in range(8):
        blk = f_in[b].astype(F32)
        out += [blk[a * OWN : (a + 1) * OWN] for a in range(SHARE)]
    dq_ref[...] = jnp.concatenate(out, axis=1).astype(BF16)

    def drain1(k, s):
        s1(k).wait_send()
        return s

    lax.fori_loop(1, 16, drain1, 0)
    for i in range(2):
        kv_copy(i, kv.at[2, i], 2, zp).wait_send()
        kv_copy(i, kv.at[1, i], 1, sib).wait_send()
        kv_copy(i, kv.at[3, i], 3, sib).wait_send()
    for way in range(3):
        for p in range(4):
            x_copy(way, p).wait_send()

    def drain_st(n, s):
        st_copy(n // 7, n % 7 + 1).wait_send()
        return s

    lax.fori_loop(0, 28, drain_st, 0)
    for k in (1, 2, 3):
        dq_copy((x + k) % 4).wait_send()

    def drain_f(k, s):
        f_copy(k).wait_send()
        return s

    lax.fori_loop(1, 8, drain_f, 0)
    c_copy.wait_send()
    z_copy.wait_send()
    zz_copy.wait_send()


def on_device(queries, grad_out, keys, values, prompt_len, resp_len):
    vmem = pl.BlockSpec(memory_space=pltpu.VMEM)
    smem = pl.BlockSpec(memory_space=pltpu.SMEM)
    hbm = pl.BlockSpec(memory_space=pl.ANY)
    dma = pltpu.SemaphoreType.DMA
    return pl.pallas_call(
        kernel,
        out_shape=[
            jax.ShapeDtypeStruct((OWN, QH * HD), BF16),
            jax.ShapeDtypeStruct((SPAN, HD), BF16),
            jax.ShapeDtypeStruct((SPAN, HD), BF16),
        ],
        in_specs=[smem, smem, vmem, vmem, hbm, hbm],
        out_specs=[vmem, vmem, vmem],
        scratch_shapes=[
            pltpu.VMEM((KH, 2 * BLK, HD), BF16),
            pltpu.VMEM((4, 16, 2 * BLK, HD), BF16),
            pltpu.VMEM((4, UNIT, HD), BF16),
            pltpu.VMEM((4, UNIT, HD), BF16),
            pltpu.VMEM((4, 2, SPAN, HD), BF16),
            pltpu.VMEM((HD, KEYS), BF16),
            pltpu.VMEM((4, KEYS, UNIT), F32),
            pltpu.VMEM((4, KEYS, UNIT), F32),
            pltpu.VMEM((4, NT, UNIT), F32),
            pltpu.VMEM((4, 8, 16, HD), F32),
            pltpu.VMEM((KEYS, HD), F32),
            pltpu.VMEM((KEYS, HD), F32),
            pltpu.VMEM((UNIT, HD), F32),
            pltpu.VMEM((4, UNIT, HD), BF16),
            pltpu.VMEM((4, UNIT, HD), BF16),
            pltpu.VMEM((UNIT // 2, HD), BF16),
            pltpu.VMEM((UNIT // 2, HD), BF16),
            pltpu.VMEM((8, BLK + 8, HD), BF16),
            pltpu.VMEM((8, BLK + 8, HD), BF16),
            pltpu.VMEM((2, 2, SPAN, HD), BF16),
            pltpu.VMEM((2, 2, SPAN, HD), BF16),
            pltpu.VMEM((2, SPAN, HD), BF16),
            pltpu.VMEM((2, SPAN, HD), BF16),
            dma((2,)),
            dma((4, 2)),
            dma((4, 2)),
            dma((16,)),
            dma((16,)),
            dma((3, 4)),
            dma((3, 4)),
            dma((4, 8)),
            dma((4, 8)),
            dma((4,)),
            dma((4,)),
            dma((2,)),
            dma((8,)),
            dma((8,)),
            dma((2,)),
            dma((2,)),
        ],
        compiler_params=pltpu.CompilerParams(
            collective_id=0, has_side_effects=True, vmem_limit_bytes=60 * 2**20
        ),
        name="window_grads",
    )(prompt_len, resp_len, queries, grad_out, keys, values)


def solution(mesh):
    in_specs = (
        P(("group", "ctx"), None),
        P(("group", "ctx"), None),
        P("ctx", None),
        P("ctx", None),
        P(),
        P("group", None),
    )
    out_specs = (P(("group", "ctx"), None), P("ctx", "group"), P("ctx", "group"))
    return jax.shard_map(
        on_device, mesh=mesh, in_specs=in_specs, out_specs=out_specs, check_vma=False
    )
```

```python
import functools
import math

import jax
import jax.numpy as jnp
from jax import lax
from jax.experimental import pallas as pl
from jax.experimental.pallas import tpu as pltpu
from jax.sharding import PartitionSpec as P

QH = 40
KH = 8
HD = 128
SHARE = QH // KH
WINDOW = 128
SPAN = 512
OWN = 8
BLK = OWN * SHARE
UNIT = 16 * BLK
KT = 256
KEYS = 4 * SPAN
NT = KEYS // KT
SCALE = 1.0 / math.sqrt(HD)
LOG2 = SCALE * math.log2(math.e)
TRANS = (((1,), (1,)), ((), ()))
MESH = pl.DeviceIdType.MESH
F32 = jnp.float32
BF16 = jnp.bfloat16


def dot(a, b):
    return jnp.dot(a, b, preferred_element_type=F32)


def dot_t(a, b):
    return lax.dot_general(a, b, TRANS, preferred_element_type=F32)


def wide(rows):
    return jnp.concatenate([rows[i : i + 1] for i in range(SHARE)], axis=1)


def tall(row):
    return jnp.concatenate([row[:, i * HD : (i + 1) * HD] for i in range(SHARE)], axis=0)


def kernel(
    plen_ref, rlen_ref, q_ref, do_ref, k_hbm, v_hbm,
    dq_ref, dk_ref, dv_ref,
    snd, held, gath, q_s, do_s, kv, k_t, e_buf, dp_buf, mst, st_loc, st_all, rdots, dka, dva, dq_acc,
    r_out, r_in, f_out, f_in, c_out, c_in, zz_out, zz_in,
    loc_sem, kv_send, kv_recv, z_send, z_recv, g_send, g_recv, st_send, st_recv,
    r_send, r_recv, f_send, f_recv, c_sem, zz_sem,
):
    g = lax.axis_index("group")
    c = lax.axis_index("ctx")
    core = c % 2
    z_lo = (c // 2) % 4
    x = c // 8
    par = z_lo % 2
    zl = z_lo // 2
    y = g // 2
    z_hi = g % 2
    zq = z_hi * 2 + zl
    pq = z_hi * 2 + 1 - zl
    order = [zq, pq, 3 - zq, 3 - pq]
    me16 = zq * 4 + y
    me8 = x * 2 + zl

    def ctx_of(x_, z_lo_, core_):
        return (x_ * 4 + z_lo_) * 2 + core_

    sib = (g, ctx_of(x, z_lo, 1 - core))
    zp_lo = z_lo + 1 - 2 * par
    zp = (g, ctx_of(x, zp_lo, core))
    mate = (g, ctx_of(x, (1 - zl) * 2 + par, core))

    def place(dest):
        z_ = dest // 4
        return ((dest % 4) * 2 + z_ // 2, ctx_of(x, (z_ % 2) * 2 + par, core))

    def ring(k):
        dest = (me8 + k) % 8
        return (g, ctx_of(dest // 2, (dest % 2) * 2 + par, core))

    def at_x(k):
        return (g, ctx_of((x + k) % 4, z_lo, core))

    def remote(src, dst, send, recv, dev):
        return pltpu.make_async_remote_copy(
            src_ref=src, dst_ref=dst, send_sem=send, recv_sem=recv, device_id=dev, device_id_type=MESH
        )

    def repeat(first, last, step):
        def body(k, s):
            step(k)
            return s

        lax.fori_loop(first, last, body, 0)

    def level(k):
        return (((y + k) % 4) * 2 + z_hi, ctx_of((x + k // 4) % 4, z_lo, core))

    barrier = pltpu.get_barrier_semaphore()

    def greet(dev):
        pl.semaphore_signal(barrier, inc=1, device_id=dev, device_id_type=MESH)

    repeat(1, 16, lambda k: greet(level(k)))
    repeat(0, 12, lambda k: greet(place((zq * 4 + 4 + k) % 16)))
    for dx in (1, 2, 3):
        greet((g, ctx_of((x + dx) % 4, (1 - zl) * 2 + par, core)))
    greet(sib)
    greet(zp)

    cols = pl.ds(pl.multiple_of(g * HD, HD), HD)
    local = [
        pltpu.make_async_copy(h.at[:, cols], kv.at[0, i], loc_sem.at[i]) for i, h in enumerate((k_hbm, v_hbm))
    ]
    for cp in local:
        cp.start()

    qf = q_ref[...].astype(F32)
    live_to = rlen_ref[0, c // 16]
    t_row = (c % 16) * OWN + lax.broadcasted_iota(jnp.int32, (OWN, 1), 0)
    dof = jnp.where(t_row < live_to, do_ref[...].astype(F32), 0.0)
    for b in range(KH):
        rows = [m[:, (b * SHARE + a) * HD : (b * SHARE + a + 1) * HD] for m in (qf, dof) for a in range(SHARE)]
        snd[b % 2, b // 2] = jnp.concatenate(rows, axis=0).astype(BF16)
    gath[zq, x * 4 + y] = snd[z_hi, y]

    pl.semaphore_wait(barrier, 32)

    def z_copy(r):
        dest = order[r]
        half = z_hi if r == 1 else 1 - z_hi
        return remote(snd.at[half], held.at[zq], z_send.at[r], z_recv.at[r], place(dest * 4 + y))

    def g_copy(r, k):
        zr = order[r]
        head = (y + k) % 4
        src = snd.at[z_hi, head] if r == 0 else held.at[zr, head]
        return remote(src, gath.at[zr, x * 4 + y], g_send.at[r], g_recv.at[r], level(k))

    def spread(r):
        if r > 0:
            z_copy(r).wait_recv()
            gath[order[r], x * 4 + y] = held[order[r], y]
        repeat(1, 16, lambda k: g_copy(r, k).start())

    def all15(r):
        part = gath.at[order[r], pl.ds(0, 15)]
        return remote(part, part, g_send.at[r], g_recv.at[r], level(1))

    z_copy(1).start()
    z_copy(2).start()
    spread(0)
    z_copy(3).start()

    def kv_copy(i, src, slot, dev):
        return remote(src, kv.at[slot, i], kv_send.at[slot, i], kv_recv.at[slot, i], dev)

    for i, h in enumerate((k_hbm, v_hbm)):
        kv_copy(i, h.at[:, cols], 1, sib).start()

    dka[...] = jnp.zeros_like(dka)
    dva[...] = jnp.zeros_like(dva)
    dq_acc[...] = jnp.zeros_like(dq_acc)
    st_loc[...] = jnp.concatenate([jnp.full((4, 1, UNIT), -1e30, F32), jnp.zeros((4, 7, UNIT), F32)], axis=1)

    spread(1)
    for i, h in enumerate((k_hbm, v_hbm)):
        kv_copy(i, h.at[:, cols], 2, zp).start()
    spread(2)
    for cp in local:
        cp.wait()
    for i in range(2):
        kv_copy(i, kv.at[1, i], 1, sib).wait_recv()

    plen = plen_ref[0]
    c_zp = zp[1]
    c_base = [c * SPAN, sib[1] * SPAN, c_zp * SPAN, (c_zp + 1 - 2 * core) * SPAN]

    def st_copy(unit, k):
        return remote(
            st_all.at[unit, me8], st_all.at[unit, me8], st_send.at[unit], st_recv.at[unit], ring(k)
        )

    def st_seven(unit):
        part = st_all.at[unit, pl.ds(0, 7)]
        return remote(part, part, st_send.at[unit], st_recv.at[unit], ring(1))

    def source(r):
        same = (1 - r // 2) * z_hi + (r // 2) * (1 - z_hi)
        mine = (1 - r % 2) * zl + (r % 2) * (1 - zl)
        return same * 2 + (1 - r // 2) * mine + (r // 2) * (1 - mine)

    def phase1(i, carry):
        unit = source(jnp.where(i < 6, i % 3, 3))
        half = jnp.where(i < 6, i // 3, i - 6)

        @pl.when(i == 0)
        def _():
            all15(0).wait_recv()

        @pl.when(i == 1)
        def _():
            spread(3)
            all15(1).wait_recv()

        @pl.when(i == 2)
        def _():
            for i_ in range(2):
                kv_copy(i_, kv.at[2, i_], 2, zp).wait_recv()
                kv_copy(i_, kv.at[2, i_], 3, sib).start()
            all15(2).wait_recv()

        @pl.when(i == 3)
        def _():
            for i_ in range(2):
                kv_copy(i_, kv.at[3, i_], 3, sib).wait_recv()

        @pl.when(i == 6)
        def _():
            all15(3).wait_recv()

        @pl.when(half == 0)
        def _():
            both = gath[unit].astype(F32)
            q_s[unit] = both[:, :BLK].reshape(UNIT, HD).astype(BF16)
            do_s[unit] = both[:, BLK:].reshape(UNIT, HD).astype(BF16)

        def cell():
            qu, dou = q_s[unit], do_s[unit]
            old = st_loc[unit]
            tops, sums, dots = [old[0:1]], [old[1:2]], [old[2:3]]
            for t in range(NT // 2):
                slot, part = half * 2 + t // 2, pl.ds(t % 2 * KT, KT)
                rows = pl.ds(pl.multiple_of(half * 2 * SPAN + t * KT, KT), KT)
                s = dot_t(kv[slot, 0, part], qu)
                if t % 2 == 1:
                    base = jnp.where(half == 0, c_base[t // 2], c_base[2 + t // 2]) + KT
                    at = base + lax.broadcasted_iota(jnp.int32, (KT, 1), 0)
                    s = jnp.where(at < plen, s, -1e30)
                dp = dot_t(kv[slot, 1, part], dou)
                top = jnp.max(s, axis=0, keepdims=True)
                e = jnp.exp2((s - top) * LOG2)
                e_buf[unit, rows] = e
                dp_buf[unit, rows] = dp
                tops.append(top)
                sums.append(jnp.sum(e, axis=0, keepdims=True))
                dots.append(jnp.sum(e * dp, axis=0, keepdims=True))
            top = functools.reduce(jnp.maximum, tops)
            total, rdot = 0.0, 0.0
            for t in range(NT // 2 + 1):
                w = jnp.exp2((tops[t] - top) * LOG2)
                total = total + sums[t] * w
                rdot = rdot + dots[t] * w
            mst[unit, half] = jnp.concatenate(tops[1:], axis=0)
            st_loc[unit, 0:3] = jnp.concatenate([top, total, rdot], axis=0)

        cell()

        @pl.when(half == 1)
        def _():
            s = st_loc[unit]
            st_all[unit, me8] = jnp.concatenate([tall(s[0:1]), tall(s[1:2]), tall(s[2:3]), jnp.zeros((1, HD), F32)], axis=0)
            repeat(1, 8, lambda k: st_copy(unit, k).start())

        return carry

    def drain_a():
        for r in range(4):
            all15(r).wait_send()
        for r in (1, 2, 3):
            z_copy(r).wait_send()
        for i in range(2):
            kv_copy(i, kv.at[2, i], 2, zp).wait_send()
            kv_copy(i, kv.at[1, i], 1, sib).wait_send()
            kv_copy(i, kv.at[3, i], 3, sib).wait_send()
        repeat(0, 4, lambda u: st_seven(u).wait_send())

    lax.fori_loop(0, 8, phase1, 0)

    for slot in range(4):
        k_t[slot // 2, :, slot % 2 * SPAN : (slot % 2 + 1) * SPAN] = kv[slot, 0].astype(F32).T.astype(BF16)

    def combine(unit):
        st_seven(unit).wait_recv()
        stats = st_all[unit]
        top = jnp.max(stats[:, 0:SHARE], axis=0)
        w = jnp.exp2((stats[:, 0:SHARE] - top[None]) * LOG2)
        total = jnp.sum(stats[:, SHARE : 2 * SHARE] * w, axis=0)
        rdot = jnp.sum(stats[:, 2 * SHARE : 3 * SHARE] * w, axis=0) / total
        top, inv = wide(top), wide(1.0 / total)
        rdots[unit] = wide(rdot)
        mst[unit] = jnp.exp2((mst[unit] - top[None]) * LOG2) * inv[None]


    c_copy = [remote(c_out.at[n], c_in.at[n], c_sem.at[0, n], c_sem.at[1, n], sib) for n in range(2)]
    zz_copy = remote(zz_out, zz_in, zz_sem.at[0], zz_sem.at[1], zp)

    def r_copy(r, k):
        dest = (x + k) % 4
        return remote(r_out.at[r, dest], r_in.at[r, x], r_send.at[r], r_recv.at[r], at_x(k))

    def r_three(r):
        part = r_in.at[r, pl.ds(0, 3)]
        return remote(part, part, r_send.at[r], r_recv.at[r], at_x(1))

    def scatter(r):
        dq = dq_acc[order[r]]
        for n in range(4):
            r_out[r, n] = dq[n * 4 * BLK : (n + 1) * 4 * BLK].astype(BF16)
        for k in (1, 2, 3):
            r_copy(r, k).start()

    def f_copy(r, k):
        head = (y + k) % 4
        return remote(f_out.at[r, head], f_in.at[me16], f_send.at[r], f_recv.at[r], place(order[r] * 4 + head))

    def f_part(r):
        count = 3 if r == 0 else 4
        part = f_in.at[pl.ds(0, count)]
        return remote(part, part, f_send.at[r], f_recv.at[r], place(order[r] * 4 + y))

    def deliver(r):
        r_three(r).wait_recv()
        tot = dq_acc[order[r], pl.ds(pl.multiple_of(x * 4 * BLK, 4 * BLK), 4 * BLK)]
        for k in (1, 2, 3):
            tot = tot + r_in[r, (x + k) % 4].astype(F32)
        pad = jnp.zeros((8, HD), F32)
        for n in range(4):
            f_out[r, n] = jnp.concatenate([tot[n * BLK : (n + 1) * BLK], pad], axis=0).astype(BF16)
        if r == 0:
            f_in[me16] = f_out[0, y]
        repeat(1 if r == 0 else 0, 4, lambda k: f_copy(r, k).start())

    def c_start(n):
        rows = pl.ds((1 + 2 * n) * SPAN, SPAN)
        c_out[n, 0] = (dka[rows] * SCALE).astype(BF16)
        c_out[n, 1] = dva[rows].astype(BF16)
        c_copy[n].start()

    def phase2(i, carry):
        r = jnp.where(i < 3, 1 - i % 2, jnp.where(i < 7, 2 + (i // 4) * (1 - i // 6), 0))
        unit = source(r)
        half = jnp.where(i < 5, 1 - (i // 2) * (1 - i // 3), 0)

        @pl.when(i < 2)
        def _():
            combine(unit)

        @pl.when((i == 3) | (i == 4))
        def _():
            combine(unit)

        def cell():
            qu, dou = q_s[unit], do_s[unit]
            factor, rdot = mst[unit, half], rdots[unit]
            dq_t = jnp.zeros((HD, UNIT), F32)
            for t in range(NT // 2):
                rows = pl.ds(pl.multiple_of(half * 2 * SPAN + t * KT, KT), KT)
                p = e_buf[unit, rows] * factor[t : t + 1]
                ds = (p * (dp_buf[unit, rows] - rdot)).astype(BF16)
                dva[rows] += dot(p.astype(BF16), dou)
                dka[rows] += dot(ds, qu)
                dq_t += dot(k_t[half, :, t * KT : (t + 1) * KT], ds)
            dq_acc[unit] += dq_t.T * SCALE

        cell()

        @pl.when(i == 2)
        def _():
            scatter(1)

        @pl.when(i == 4)
        def _():
            c_start(1)

        @pl.when(i == 5)
        def _():
            scatter(3)
            c_copy[1].wait_recv()
            far = pl.ds(2 * SPAN, SPAN)
            zz_out[0] = (dka[far] * SCALE + c_in[1, 0].astype(F32)).astype(BF16)
            zz_out[1] = (dva[far] + c_in[1, 1].astype(F32)).astype(BF16)
            zz_copy.start()

        @pl.when(i == 6)
        def _():
            scatter(2)
            deliver(1)

        return carry

    lax.fori_loop(0, 8, phase2, 0)
    scatter(0)
    c_start(0)
    deliver(3)
    deliver(2)
    deliver(0)

    c_copy[0].wait_recv()
    near = pl.ds(0, SPAN)
    dka[near] = dka[near] * SCALE + c_in[0, 0].astype(F32)
    dva[near] = dva[near] + c_in[0, 1].astype(F32)
    zz_copy.wait_recv()
    dk_ref[...] = (dka[near] + zz_in[0].astype(F32)).astype(BF16)
    dv_ref[...] = (dva[near] + zz_in[1].astype(F32)).astype(BF16)

    for r in range(4):
        f_part(r).wait_recv()
    out = []
    for b in range(KH):
        first = (b % 2) * 8 + b // 2
        blk = f_in[first].astype(F32) + f_in[first + 4].astype(F32)
        out += [blk[a * OWN : (a + 1) * OWN] for a in range(SHARE)]
    dq_ref[...] = jnp.concatenate(out, axis=1).astype(BF16)

    drain_a()
    for n in range(2):
        c_copy[n].wait_send()
    zz_copy.wait_send()
    for r in range(4):
        r_three(r).wait_send()
        f_part(r).wait_send()


def on_device(queries, grad_out, keys, values, prompt_len, resp_len):
    vmem = pl.BlockSpec(memory_space=pltpu.VMEM)
    smem = pl.BlockSpec(memory_space=pltpu.SMEM)
    hbm = pl.BlockSpec(memory_space=pl.ANY)
    dma = pltpu.SemaphoreType.DMA
    return pl.pallas_call(
        kernel,
        out_shape=[
            jax.ShapeDtypeStruct((OWN, QH * HD), BF16),
            jax.ShapeDtypeStruct((SPAN, HD), BF16),
            jax.ShapeDtypeStruct((SPAN, HD), BF16),
        ],
        in_specs=[smem, smem, vmem, vmem, hbm, hbm],
        out_specs=[vmem, vmem, vmem],
        scratch_shapes=[
            pltpu.VMEM((2, 4, 2 * BLK, HD), BF16),
            pltpu.VMEM((4, 4, 2 * BLK, HD), BF16),
            pltpu.VMEM((4, 16, 2 * BLK, HD), BF16),
            pltpu.VMEM((4, UNIT, HD), BF16),
            pltpu.VMEM((4, UNIT, HD), BF16),
            pltpu.VMEM((4, 2, SPAN, HD), BF16),
            pltpu.VMEM((2, HD, 2 * SPAN), BF16),
            pltpu.VMEM((4, KEYS, UNIT), F32),
            pltpu.VMEM((4, KEYS, UNIT), F32),
            pltpu.VMEM((4, 2, NT // 2, UNIT), F32),
            pltpu.VMEM((4, 8, UNIT), F32),
            pltpu.VMEM((4, 8, 16, HD), F32),
            pltpu.VMEM((4, 1, UNIT), F32),
            pltpu.VMEM((KEYS, HD), F32),
            pltpu.VMEM((KEYS, HD), F32),
            pltpu.VMEM((4, UNIT, HD), F32),
            pltpu.VMEM((4, 4, 4 * BLK, HD), BF16),
            pltpu.VMEM((4, 4, 4 * BLK, HD), BF16),
            pltpu.VMEM((4, 4, BLK + 8, HD), BF16),
            pltpu.VMEM((16, BLK + 8, HD), BF16),
            pltpu.VMEM((2, 2, SPAN, HD), BF16),
            pltpu.VMEM((2, 2, SPAN, HD), BF16),
            pltpu.VMEM((2, SPAN, HD), BF16),
            pltpu.VMEM((2, SPAN, HD), BF16),
            dma((2,)),
            dma((4, 2)),
            dma((4, 2)),
            dma((4,)),
            dma((4,)),
            dma((4,)),
            dma((4,)),
            dma((4,)),
            dma((4,)),
            dma((4,)),
            dma((4,)),
            dma((4,)),
            dma((4,)),
            dma((2, 2)),
            dma((2,)),
        ],
        compiler_params=pltpu.CompilerParams(
            collective_id=0, has_side_effects=True, vmem_limit_bytes=60 * 2**20
        ),
        name="window_grads",
    )(prompt_len, resp_len, queries, grad_out, keys, values)


def solution(mesh):
    in_specs = (
        P(("group", "ctx"), None),
        P(("group", "ctx"), None),
        P("ctx", None),
        P("ctx", None),
        P(),
        P("group", None),
    )
    out_specs = (P(("group", "ctx"), None), P("ctx", "group"), P("ctx", "group"))
    return jax.shard_map(
        on_device, mesh=mesh, in_specs=in_specs, out_specs=out_specs, check_vma=False
    )
```

```python
import functools
import math

import jax
import jax.numpy as jnp
from jax import lax
from jax.experimental import pallas as pl
from jax.experimental.pallas import tpu as pltpu
from jax.sharding import PartitionSpec as P

QH = 40
KH = 8
HD = 128
SHARE = QH // KH
WINDOW = 128
SPAN = 512
OWN = 8
BLK = OWN * SHARE
UNIT = 16 * BLK
KT = 256
KEYS = 4 * SPAN
NT = KEYS // KT
SCALE = 1.0 / math.sqrt(HD)
LOG2 = SCALE * math.log2(math.e)
TRANS = (((1,), (1,)), ((), ()))
MESH = pl.DeviceIdType.MESH
F32 = jnp.float32
BF16 = jnp.bfloat16


def dot(a, b):
    return jnp.dot(a, b, preferred_element_type=F32)


def dot_t(a, b):
    return lax.dot_general(a, b, TRANS, preferred_element_type=F32)


def wide(rows):
    return jnp.concatenate([rows[i : i + 1] for i in range(SHARE)], axis=1)


def tall(row):
    return jnp.concatenate([row[:, i * HD : (i + 1) * HD] for i in range(SHARE)], axis=0)


def kernel(
    plen_ref, rlen_ref, q_hbm, do_hbm, k_hbm, v_hbm,
    f_in, dk_ref, dv_ref,
    q_ref, do_ref, snd, held, gath, q_s, do_s, kv, k_t, e_buf, dp_buf, mst, st_loc, st_all, rdots, dka, dva, dq_acc,
    r_out, r_in, f_out, c_out, c_in, zz_out, zz_in,
    loc_sem, kv_send, kv_recv, z_send, z_recv, g_send, g_recv, st_send, st_recv,
    r_send, r_recv, f_send, f_recv, c_sem, zz_sem,
):
    g = lax.axis_index("group")
    c = lax.axis_index("ctx")
    core = c % 2
    z_lo = (c // 2) % 4
    x = c // 8
    par = z_lo % 2
    zl = z_lo // 2
    y = g // 2
    z_hi = g % 2
    zq = z_hi * 2 + zl
    pq = z_hi * 2 + 1 - zl
    order = [zq, pq, 3 - zq, 3 - pq]
    me16 = zq * 4 + y
    me8 = x * 2 + zl

    def ctx_of(x_, z_lo_, core_):
        return (x_ * 4 + z_lo_) * 2 + core_

    sib = (g, ctx_of(x, z_lo, 1 - core))
    zp_lo = z_lo + 1 - 2 * par
    zp = (g, ctx_of(x, zp_lo, core))
    mate = (g, ctx_of(x, (1 - zl) * 2 + par, core))

    def place(dest):
        z_ = dest // 4
        return ((dest % 4) * 2 + z_ // 2, ctx_of(x, (z_ % 2) * 2 + par, core))

    def ring(k):
        dest = (me8 + k) % 8
        return (g, ctx_of(dest // 2, (dest % 2) * 2 + par, core))

    def at_x(k):
        return (g, ctx_of((x + k) % 4, z_lo, core))

    def remote(src, dst, send, recv, dev):
        return pltpu.make_async_remote_copy(
            src_ref=src, dst_ref=dst, send_sem=send, recv_sem=recv, device_id=dev, device_id_type=MESH
        )

    def repeat(first, last, step):
        def body(k, s):
            step(k)
            return s

        lax.fori_loop(first, last, body, 0)

    def level(k):
        return (((y + k) % 4) * 2 + z_hi, ctx_of((x + k // 4) % 4, z_lo, core))

    loads = [pltpu.make_async_copy(a, b, loc_sem.at[2 + i]) for i, (a, b) in enumerate(((q_hbm, q_ref), (do_hbm, do_ref)))]
    for cp in loads:
        cp.start()

    barrier = pltpu.get_barrier_semaphore()

    def greet(dev):
        pl.semaphore_signal(barrier, inc=1, device_id=dev, device_id_type=MESH)

    repeat(1, 16, lambda k: greet(level(k)))
    repeat(0, 12, lambda k: greet(place((zq * 4 + 4 + k) % 16)))
    for dx in (1, 2, 3):
        greet((g, ctx_of((x + dx) % 4, (1 - zl) * 2 + par, core)))
    greet(sib)
    greet(zp)

    cols = pl.ds(pl.multiple_of(g * HD, HD), HD)
    local = [
        pltpu.make_async_copy(h.at[:, cols], kv.at[0, i], loc_sem.at[i]) for i, h in enumerate((k_hbm, v_hbm))
    ]
    for cp in local:
        cp.start()

    for cp in loads:
        cp.wait()
    qf = q_ref[...].astype(F32)
    live_to = rlen_ref[0, c // 16]
    t_row = (c % 16) * OWN + lax.broadcasted_iota(jnp.int32, (OWN, 1), 0)
    dof = jnp.where(t_row < live_to, do_ref[...].astype(F32), 0.0)
    for b in range(KH):
        rows = [m[:, (b * SHARE + a) * HD : (b * SHARE + a + 1) * HD] for m in (qf, dof) for a in range(SHARE)]
        snd[b % 2, b // 2] = jnp.concatenate(rows, axis=0).astype(BF16)
    gath[zq, x * 4 + y] = snd[z_hi, y]

    pl.semaphore_wait(barrier, 32)

    def z_copy(r):
        if r == 3:
            part = held.at[order[2]]
            return remote(part, part, z_send.at[3], z_recv.at[3], mate)
        half = z_hi if r == 1 else 1 - z_hi
        return remote(snd.at[half], held.at[zq], z_send.at[r], z_recv.at[r], place(order[r] * 4 + y))

    def g_copy(r, k):
        zr = order[r]
        head = (y + k) % 4
        src = snd.at[z_hi, head] if r == 0 else held.at[zr, head]
        return remote(src, gath.at[zr, x * 4 + y], g_send.at[r], g_recv.at[r], level(k))

    def spread(r):
        if r > 0:
            z_copy(r).wait_recv()
            if r == 2:
                z_copy(3).start()
            gath[order[r], x * 4 + y] = held[order[r], y]
        repeat(1, 16, lambda k: g_copy(r, k).start())

    def all15(r):
        part = gath.at[order[r], pl.ds(0, 15)]
        return remote(part, part, g_send.at[r], g_recv.at[r], level(1))

    z_copy(1).start()
    z_copy(2).start()
    spread(0)

    def kv_copy(i, src, slot, dev):
        return remote(src, kv.at[slot, i], kv_send.at[slot, i], kv_recv.at[slot, i], dev)

    for i, h in enumerate((k_hbm, v_hbm)):
        kv_copy(i, h.at[:, cols], 1, sib).start()
        kv_copy(i, h.at[:, cols], 2, zp).start()

    dka[...] = jnp.zeros_like(dka)
    dva[...] = jnp.zeros_like(dva)
    st_loc[...] = jnp.concatenate([jnp.full((4, 1, UNIT), -1e30, F32), jnp.zeros((4, 7, UNIT), F32)], axis=1)

    spread(1)
    spread(2)
    for cp in local:
        cp.wait()
    for i in range(2):
        kv_copy(i, kv.at[1, i], 1, sib).wait_recv()

    def turn(slot):
        k_t[slot // 2, :, slot % 2 * SPAN : (slot % 2 + 1) * SPAN] = kv[slot, 0].astype(F32).T.astype(BF16)

    turn(0)
    turn(1)
    plen = plen_ref[0]
    c_zp = zp[1]
    c_base = [c * SPAN, sib[1] * SPAN, c_zp * SPAN, (c_zp + 1 - 2 * core) * SPAN]

    def st_copy(unit, k):
        return remote(
            st_all.at[unit, me8], st_all.at[unit, me8], st_send.at[unit], st_recv.at[unit], ring(k)
        )

    def st_seven(unit):
        part = st_all.at[unit, pl.ds(0, 7)]
        return remote(part, part, st_send.at[unit], st_recv.at[unit], ring(1))

    def source(r):
        same = (1 - r // 2) * z_hi + (r // 2) * (1 - z_hi)
        mine = (1 - r % 2) * zl + (r % 2) * (1 - zl)
        return same * 2 + (1 - r // 2) * mine + (r // 2) * (1 - mine)

    def phase1(i, carry):
        unit, half = source(i // 2), i % 2

        @pl.when(i == 0)
        def _():
            all15(0).wait_recv()

        @pl.when(i == 1)
        def _():
            for i_ in range(2):
                kv_copy(i_, kv.at[2, i_], 2, zp).wait_recv()
                kv_copy(i_, kv.at[2, i_], 3, sib).start()
            spread(3)
            turn(2)
            for i_ in range(2):
                kv_copy(i_, kv.at[3, i_], 3, sib).wait_recv()
            turn(3)

        @pl.when(i == 2)
        def _():
            all15(1).wait_recv()

        @pl.when(i == 4)
        def _():
            all15(2).wait_recv()

        @pl.when(i == 6)
        def _():
            all15(3).wait_recv()

        @pl.when(half == 0)
        def _():
            both = gath[unit].astype(F32)
            q_s[unit] = both[:, :BLK].reshape(UNIT, HD).astype(BF16)
            do_s[unit] = both[:, BLK:].reshape(UNIT, HD).astype(BF16)

        def cell():
            qu, dou = q_s[unit], do_s[unit]
            old = st_loc[unit]
            tops, sums, dots = [old[0:1]], [old[1:2]], [old[2:3]]
            for t in range(NT // 2):
                slot, part = half * 2 + t // 2, pl.ds(t % 2 * KT, KT)
                rows = pl.ds(pl.multiple_of(half * 2 * SPAN + t * KT, KT), KT)
                s = dot_t(kv[slot, 0, part], qu)
                if t % 2 == 1:
                    base = jnp.where(half == 0, c_base[t // 2], c_base[2 + t // 2]) + KT
                    at = base + lax.broadcasted_iota(jnp.int32, (KT, 1), 0)
                    s = jnp.where(at < plen, s, -1e30)
                dp = dot_t(kv[slot, 1, part], dou)
                top = jnp.max(s, axis=0, keepdims=True)
                e = jnp.exp2((s - top) * LOG2)
                e_buf[unit, rows] = e
                dp_buf[unit, rows] = dp
                tops.append(top)
                sums.append(jnp.sum(e, axis=0, keepdims=True))
                dots.append(jnp.sum(e * dp, axis=0, keepdims=True))
            top = functools.reduce(jnp.maximum, tops)
            total, rdot = 0.0, 0.0
            for t in range(NT // 2 + 1):
                w = jnp.exp2((tops[t] - top) * LOG2)
                total = total + sums[t] * w
                rdot = rdot + dots[t] * w
            mst[unit, half] = jnp.concatenate(tops[1:], axis=0)
            st_loc[unit, 0:3] = jnp.concatenate([top, total, rdot], axis=0)

        cell()

        @pl.when(half == 1)
        def _():
            s = st_loc[unit]
            st_all[unit, me8] = jnp.concatenate([tall(s[0:1]), tall(s[1:2]), tall(s[2:3]), jnp.zeros((1, HD), F32)], axis=0)
            repeat(1, 8, lambda k: st_copy(unit, k).start())

        return carry

    def drain_a():
        for r in range(4):
            all15(r).wait_send()
        for r in (1, 2, 3):
            z_copy(r).wait_send()
        for i in range(2):
            kv_copy(i, kv.at[2, i], 2, zp).wait_send()
            kv_copy(i, kv.at[1, i], 1, sib).wait_send()
            kv_copy(i, kv.at[3, i], 3, sib).wait_send()
        repeat(0, 4, lambda u: st_seven(u).wait_send())

    lax.fori_loop(0, 8, phase1, 0)

    def combine(unit):
        st_seven(unit).wait_recv()
        stats = st_all[unit]
        top = jnp.max(stats[:, 0:SHARE], axis=0)
        w = jnp.exp2((stats[:, 0:SHARE] - top[None]) * LOG2)
        total = jnp.sum(stats[:, SHARE : 2 * SHARE] * w, axis=0)
        rdot = jnp.sum(stats[:, 2 * SHARE : 3 * SHARE] * w, axis=0) / total
        top, inv = wide(top), wide(1.0 / total)
        rdots[unit] = wide(rdot)
        mst[unit] = jnp.exp2((mst[unit] - top[None]) * LOG2) * inv[None]


    c_copy = [remote(c_out.at[n], c_in.at[n], c_sem.at[0, n], c_sem.at[1, n], sib) for n in range(2)]
    zz_copy = remote(zz_out, zz_in, zz_sem.at[0], zz_sem.at[1], zp)

    def r_copy(r, k):
        dest = (x + k) % 4
        return remote(r_out.at[r, dest], r_in.at[r, x], r_send.at[r], r_recv.at[r], at_x(k))

    def r_three(r):
        part = r_in.at[r, pl.ds(0, 3)]
        return remote(part, part, r_send.at[r], r_recv.at[r], at_x(1))

    def scatter(r):
        dq = dq_acc[source(r)]
        for n in range(4):
            r_out[r, n] = dq[n * 4 * BLK : (n + 1) * 4 * BLK].astype(BF16)
        for k in (1, 2, 3):
            r_copy(r, k).start()

    def f_copy(r, k):
        head = (y + k) % 4
        return remote(f_out.at[r, head], f_in.at[me16], f_send.at[r], f_recv.at[r], place(order[r] * 4 + head))

    def f_part(r):
        count = 3 if r == 0 else 4
        part = f_in.at[pl.ds(0, count)]
        return remote(part, part, f_send.at[r], f_recv.at[r], place(order[r] * 4 + y))

    def deliver(r):
        r_three(r).wait_recv()
        tot = dq_acc[order[r], pl.ds(pl.multiple_of(x * 4 * BLK, 4 * BLK), 4 * BLK)]
        for k in (1, 2, 3):
            tot = tot + r_in[r, (x + k) % 4].astype(F32)
        pad = jnp.zeros((8, HD), F32)
        for n in range(4):
            f_out[r, n] = jnp.concatenate([tot[n * BLK : (n + 1) * BLK], pad], axis=0).astype(BF16)
        if r == 0:
            f_in[me16] = f_out[0, y]
        repeat(1 if r == 0 else 0, 4, lambda k: f_copy(r, k).start())

    def c_start(n):
        rows = pl.ds((1 + 2 * n) * SPAN, SPAN)
        c_out[n, 0] = (dka[rows] * SCALE).astype(BF16)
        c_out[n, 1] = dva[rows].astype(BF16)
        c_copy[n].start()

    def q_step(n):
        r = n + 1 - 2 * (n % 2)
        unit = source(r)
        combine(unit)
        rdot = rdots[unit]
        dq_t = jnp.zeros((HD, UNIT), F32)
        for t in range(NT):
            rows = pl.ds(t * KT, KT)
            p = e_buf[unit, rows] * mst[unit, t // 4, t % 4 : t % 4 + 1]
            ds = p * (dp_buf[unit, rows] - rdot)
            dp_buf[unit, rows] = ds
            dq_t += dot(k_t[t // 4, :, t % 4 * KT : (t % 4 + 1) * KT], ds.astype(BF16))
        dq_acc[unit] = dq_t.T * SCALE
        scatter(r)

    def kv_step(unit, half):
        qu, dou, factor = q_s[unit], do_s[unit], mst[unit, half]
        for t in range(NT // 2):
            rows = pl.ds(half * 2 * SPAN + t * KT, KT)
            p = (e_buf[unit, rows] * factor[t : t + 1]).astype(BF16)
            dva[rows] += dot(p, dou)
            dka[rows] += dot(dp_buf[unit, rows].astype(BF16), qu)

    repeat(0, 2, q_step)
    repeat(0, 2, lambda n: kv_step(source(n), 1))
    repeat(2, 4, q_step)
    deliver(1)
    deliver(0)
    repeat(2, 4, lambda n: kv_step(source(n), 1))
    c_start(1)

    def near_step(n):
        kv_step(source(n), 0)

        @pl.when(n == 0)
        def _():
            c_copy[1].wait_recv()
            far = pl.ds(2 * SPAN, SPAN)
            zz_out[0] = (dka[far] * SCALE + c_in[1, 0].astype(F32)).astype(BF16)
            zz_out[1] = (dva[far] + c_in[1, 1].astype(F32)).astype(BF16)

        @pl.when(n == 1)
        def _():
            deliver(3)

        @pl.when(n == 2)
        def _():
            deliver(2)
            zz_copy.start()

    repeat(0, 4, near_step)
    c_start(0)

    c_copy[0].wait_recv()
    near = pl.ds(0, SPAN)
    dka[near] = dka[near] * SCALE + c_in[0, 0].astype(F32)
    dva[near] = dva[near] + c_in[0, 1].astype(F32)
    zz_copy.wait_recv()
    dk_ref[...] = (dka[near] + zz_in[0].astype(F32)).astype(BF16)
    dv_ref[...] = (dva[near] + zz_in[1].astype(F32)).astype(BF16)

    for r in range(4):
        f_part(r).wait_recv()

    drain_a()
    for n in range(2):
        c_copy[n].wait_send()
    zz_copy.wait_send()
    for r in range(4):
        r_three(r).wait_send()
        f_part(r).wait_send()


def assemble(f_ref, dk_in, dv_in, dq_ref, dk_ref, dv_ref):
    out = []
    for b in range(KH):
        first = (b % 2) * 8 + b // 2
        blk = f_ref[first].astype(F32) + f_ref[first + 4].astype(F32)
        out += [blk[a * OWN : (a + 1) * OWN] for a in range(SHARE)]
    dq_ref[...] = jnp.concatenate(out, axis=1).astype(BF16)
    dk_ref[...] = dk_in[...]
    dv_ref[...] = dv_in[...]


def on_device(queries, grad_out, keys, values, prompt_len, resp_len):
    vmem = pl.BlockSpec(memory_space=pltpu.VMEM)
    smem = pl.BlockSpec(memory_space=pltpu.SMEM)
    hbm = pl.BlockSpec(memory_space=pl.ANY)
    dma = pltpu.SemaphoreType.DMA
    parts = pl.pallas_call(
        kernel,
        out_shape=[
            jax.ShapeDtypeStruct((16, BLK + 8, HD), BF16),
            jax.ShapeDtypeStruct((SPAN, HD), BF16),
            jax.ShapeDtypeStruct((SPAN, HD), BF16),
        ],
        in_specs=[smem, smem, hbm, hbm, hbm, hbm],
        out_specs=[vmem, vmem, vmem],
        scratch_shapes=[
            pltpu.VMEM((OWN, QH * HD), BF16),
            pltpu.VMEM((OWN, QH * HD), BF16),
            pltpu.VMEM((2, 4, 2 * BLK, HD), BF16),
            pltpu.VMEM((4, 4, 2 * BLK, HD), BF16),
            pltpu.VMEM((4, 16, 2 * BLK, HD), BF16),
            pltpu.VMEM((4, UNIT, HD), BF16),
            pltpu.VMEM((4, UNIT, HD), BF16),
            pltpu.VMEM((4, 2, SPAN, HD), BF16),
            pltpu.VMEM((2, HD, 2 * SPAN), BF16),
            pltpu.VMEM((4, KEYS, UNIT), F32),
            pltpu.VMEM((4, KEYS, UNIT), F32),
            pltpu.VMEM((4, 2, NT // 2, UNIT), F32),
            pltpu.VMEM((4, 8, UNIT), F32),
            pltpu.VMEM((4, 8, 16, HD), F32),
            pltpu.VMEM((4, 1, UNIT), F32),
            pltpu.VMEM((KEYS, HD), F32),
            pltpu.VMEM((KEYS, HD), F32),
            pltpu.VMEM((4, UNIT, HD), F32),
            pltpu.VMEM((4, 4, 4 * BLK, HD), BF16),
            pltpu.VMEM((4, 4, 4 * BLK, HD), BF16),
            pltpu.VMEM((4, 4, BLK + 8, HD), BF16),
            pltpu.VMEM((2, 2, SPAN, HD), BF16),
            pltpu.VMEM((2, 2, SPAN, HD), BF16),
            pltpu.VMEM((2, SPAN, HD), BF16),
            pltpu.VMEM((2, SPAN, HD), BF16),
            dma((4,)),
            dma((4, 2)),
            dma((4, 2)),
            dma((4,)),
            dma((4,)),
            dma((4,)),
            dma((4,)),
            dma((4,)),
            dma((4,)),
            dma((4,)),
            dma((4,)),
            dma((4,)),
            dma((4,)),
            dma((2, 2)),
            dma((2,)),
        ],
        compiler_params=pltpu.CompilerParams(
            collective_id=0, has_side_effects=True, vmem_limit_bytes=60 * 2**20
        ),
        name="window_grads",
    )(prompt_len, resp_len, queries, grad_out, keys, values)
    return pl.pallas_call(
        assemble,
        out_shape=[
            jax.ShapeDtypeStruct((OWN, QH * HD), BF16),
            jax.ShapeDtypeStruct((SPAN, HD), BF16),
            jax.ShapeDtypeStruct((SPAN, HD), BF16),
        ],
        in_specs=[vmem] * 3,
        out_specs=[vmem] * 3,
        name="assemble",
    )(*parts)


def solution(mesh):
    in_specs = (
        P(("group", "ctx"), None),
        P(("group", "ctx"), None),
        P("ctx", None),
        P("ctx", None),
        P(),
        P("group", None),
    )
    out_specs = (P(("group", "ctx"), None), P("ctx", "group"), P("ctx", "group"))
    return jax.shard_map(
        on_device, mesh=mesh, in_specs=in_specs, out_specs=out_specs, check_vma=False
    )
```

```python
import functools
import math

import jax
import jax.numpy as jnp
from jax import lax
from jax.experimental import pallas as pl
from jax.experimental.pallas import tpu as pltpu
from jax.sharding import PartitionSpec as P

QH = 40
KH = 8
HD = 128
SHARE = QH // KH
WINDOW = 128
SPAN = 512
OWN = 8
BLK = OWN * SHARE
UNIT = 16 * BLK
KT = 256
KEYS = 4 * SPAN
NT = KEYS // KT
SCALE = 1.0 / math.sqrt(HD)
LOG2 = SCALE * math.log2(math.e)
TRANS = (((1,), (1,)), ((), ()))
MESH = pl.DeviceIdType.MESH
F32 = jnp.float32
BF16 = jnp.bfloat16


def dot(a, b):
    return jnp.dot(a, b, preferred_element_type=F32)


def dot_t(a, b):
    return lax.dot_general(a, b, TRANS, preferred_element_type=F32)


def wide(rows):
    return jnp.concatenate([rows[i : i + 1] for i in range(SHARE)], axis=1)


def tall(row):
    return jnp.concatenate([row[:, i * HD : (i + 1) * HD] for i in range(SHARE)], axis=0)


def kernel(
    plen_ref, rlen_ref, q_hbm, do_hbm, k_hbm, v_hbm,
    f_in, dk_hbm, dv_hbm,
    q_ref, do_ref, snd, held, gath, q_s, do_s, kv, k_t, e_buf, dp_buf, mst, st_loc, st_all, rdots, dka, dva, dq_acc,
    r_out, r_in, f_out, c_out, c_in, zz_out, zz_in, done,
    loc_sem, kv_send, kv_recv, z_send, z_recv, g_send, g_recv, st_send, st_recv,
    r_send, r_recv, f_send, f_recv, c_sem, zz_sem,
):
    g = lax.axis_index("group")
    c = lax.axis_index("ctx")
    core = c % 2
    z_lo = (c // 2) % 4
    x = c // 8
    par = z_lo % 2
    zl = z_lo // 2
    y = g // 2
    z_hi = g % 2
    zq = z_hi * 2 + zl
    pq = z_hi * 2 + 1 - zl
    order = [zq, pq, 3 - zq, 3 - pq]
    me16 = zq * 4 + y
    me8 = x * 2 + zl

    def ctx_of(x_, z_lo_, core_):
        return (x_ * 4 + z_lo_) * 2 + core_

    sib = (g, ctx_of(x, z_lo, 1 - core))
    zp_lo = z_lo + 1 - 2 * par
    zp = (g, ctx_of(x, zp_lo, core))
    mate = (g, ctx_of(x, (1 - zl) * 2 + par, core))

    def place(dest):
        z_ = dest // 4
        return ((dest % 4) * 2 + z_ // 2, ctx_of(x, (z_ % 2) * 2 + par, core))

    def ring(k):
        dest = (me8 + k) % 8
        return (g, ctx_of(dest // 2, (dest % 2) * 2 + par, core))

    def at_x(k):
        return (g, ctx_of((x + k) % 4, z_lo, core))

    def remote(src, dst, send, recv, dev):
        return pltpu.make_async_remote_copy(
            src_ref=src, dst_ref=dst, send_sem=send, recv_sem=recv, device_id=dev, device_id_type=MESH
        )

    def repeat(first, last, step):
        def body(k, s):
            step(k)
            return s

        lax.fori_loop(first, last, body, 0)

    def level(k):
        return (((y + k) % 4) * 2 + z_hi, ctx_of((x + k // 4) % 4, z_lo, core))

    loads = [pltpu.make_async_copy(a, b, loc_sem.at[2 + i]) for i, (a, b) in enumerate(((q_hbm, q_ref), (do_hbm, do_ref)))]
    for cp in loads:
        cp.start()

    barrier = pltpu.get_barrier_semaphore()

    def greet(dev):
        pl.semaphore_signal(barrier, inc=1, device_id=dev, device_id_type=MESH)

    repeat(1, 16, lambda k: greet(level(k)))
    repeat(0, 12, lambda k: greet(place((zq * 4 + 4 + k) % 16)))
    for dx in (1, 2, 3):
        greet((g, ctx_of((x + dx) % 4, (1 - zl) * 2 + par, core)))
    greet(sib)
    greet(zp)

    cols = pl.ds(pl.multiple_of(g * HD, HD), HD)
    local = [
        pltpu.make_async_copy(h.at[:, cols], kv.at[0, i], loc_sem.at[i]) for i, h in enumerate((k_hbm, v_hbm))
    ]
    for cp in local:
        cp.start()

    for cp in loads:
        cp.wait()
    qf = q_ref[...].astype(F32)
    live_to = rlen_ref[0, c // 16]
    t_row = (c % 16) * OWN + lax.broadcasted_iota(jnp.int32, (OWN, 1), 0)
    dof = jnp.where(t_row < live_to, do_ref[...].astype(F32), 0.0)
    for b in range(KH):
        rows = [m[:, (b * SHARE + a) * HD : (b * SHARE + a + 1) * HD] for m in (qf, dof) for a in range(SHARE)]
        snd[b % 2, b // 2] = jnp.concatenate(rows, axis=0).astype(BF16)
    gath[zq, x * 4 + y] = snd[z_hi, y]

    pl.semaphore_wait(barrier, 32)

    def z_copy(r, j):
        head = (y + j) % 4
        if r == 3:
            part = held.at[order[2], head]
            return remote(part, part, z_send.at[3, head], z_recv.at[3, head], mate)
        half = z_hi if r == 1 else 1 - z_hi
        dev = place(order[r] * 4 + y)
        return remote(snd.at[half, head], held.at[zq, head], z_send.at[r, head], z_recv.at[r, head], dev)

    def g_copy(r, j, dx):
        zr = order[r]
        head = (y + j) % 4
        src = snd.at[z_hi, head] if r == 0 else held.at[zr, head]
        return remote(src, gath.at[zr, x * 4 + y], g_send.at[r], g_recv.at[r], level(dx * 4 + j))

    def spread(r):
        for j in range(4):
            if r > 0:
                z_copy(r, j).wait_recv()
            if r == 2:
                z_copy(3, j).start()
            if r > 0 and j == 0:
                gath[order[r], x * 4 + y] = held[order[r], y]
            repeat(1 if j == 0 else 0, 4, lambda dx: g_copy(r, j, dx).start())

    def all15(r):
        part = gath.at[order[r], pl.ds(0, 15)]
        return remote(part, part, g_send.at[r], g_recv.at[r], level(1))

    for j in range(4):
        z_copy(1, j).start()
    for j in range(4):
        z_copy(2, j).start()
    spread(0)

    def kv_copy(i, src, slot, dev):
        return remote(src, kv.at[slot, i], kv_send.at[slot, i], kv_recv.at[slot, i], dev)

    for i, h in enumerate((k_hbm, v_hbm)):
        kv_copy(i, h.at[:, cols], 1, sib).start()
        kv_copy(i, h.at[:, cols], 2, zp).start()

    dka[...] = jnp.zeros_like(dka)
    dva[...] = jnp.zeros_like(dva)
    st_loc[...] = jnp.concatenate([jnp.full((4, 1, UNIT), -1e30, F32), jnp.zeros((4, 7, UNIT), F32)], axis=1)

    spread(1)
    spread(2)
    for cp in local:
        cp.wait()
    for i in range(2):
        kv_copy(i, kv.at[1, i], 1, sib).wait_recv()

    def turn(slot):
        k_t[slot // 2, :, slot % 2 * SPAN : (slot % 2 + 1) * SPAN] = kv[slot, 0].astype(F32).T.astype(BF16)

    turn(0)
    turn(1)
    plen = plen_ref[0]
    c_zp = zp[1]
    c_base = [c * SPAN, sib[1] * SPAN, c_zp * SPAN, (c_zp + 1 - 2 * core) * SPAN]

    def st_copy(unit, k):
        return remote(
            st_all.at[unit, me8], st_all.at[unit, me8], st_send.at[unit], st_recv.at[unit], ring(k)
        )

    def st_seven(unit):
        part = st_all.at[unit, pl.ds(0, 7)]
        return remote(part, part, st_send.at[unit], st_recv.at[unit], ring(1))

    def source(r):
        same = (1 - r // 2) * z_hi + (r // 2) * (1 - z_hi)
        mine = (1 - r % 2) * zl + (r % 2) * (1 - zl)
        return same * 2 + (1 - r // 2) * mine + (r // 2) * (1 - mine)

    def phase1(i, carry):
        unit, half = source(i // 2), i % 2

        @pl.when(i == 0)
        def _():
            all15(0).wait_recv()

        @pl.when(i == 1)
        def _():
            for i_ in range(2):
                kv_copy(i_, kv.at[2, i_], 2, zp).wait_recv()
                kv_copy(i_, kv.at[2, i_], 3, sib).start()
            spread(3)
            turn(2)
            for i_ in range(2):
                kv_copy(i_, kv.at[3, i_], 3, sib).wait_recv()
            turn(3)

        @pl.when(i == 2)
        def _():
            all15(1).wait_recv()

        @pl.when(i == 4)
        def _():
            all15(2).wait_recv()

        @pl.when(i == 6)
        def _():
            all15(3).wait_recv()

        @pl.when(half == 0)
        def _():
            both = gath[unit].astype(F32)
            q_s[unit] = both[:, :BLK].reshape(UNIT, HD).astype(BF16)
            do_s[unit] = both[:, BLK:].reshape(UNIT, HD).astype(BF16)

        def cell():
            qu, dou = q_s[unit], do_s[unit]
            old = st_loc[unit]
            tops, sums, dots = [old[0:1]], [old[1:2]], [old[2:3]]
            for t in range(NT // 2):
                slot, part = half * 2 + t // 2, pl.ds(t % 2 * KT, KT)
                rows = pl.ds(pl.multiple_of(half * 2 * SPAN + t * KT, KT), KT)
                s = dot_t(kv[slot, 0, part], qu)
                if t % 2 == 1:
                    base = jnp.where(half == 0, c_base[t // 2], c_base[2 + t // 2]) + KT
                    at = base + lax.broadcasted_iota(jnp.int32, (KT, 1), 0)
                    s = jnp.where(at < plen, s, -1e30)
                dp = dot_t(kv[slot, 1, part], dou)
                top = jnp.max(s, axis=0, keepdims=True)
                e = jnp.exp2((s - top) * LOG2)
                e_buf[unit, rows] = e
                dp_buf[unit, rows] = dp
                tops.append(top)
                sums.append(jnp.sum(e, axis=0, keepdims=True))
                dots.append(jnp.sum(e * dp, axis=0, keepdims=True))
            top = functools.reduce(jnp.maximum, tops)
            total, rdot = 0.0, 0.0
            for t in range(NT // 2 + 1):
                w = jnp.exp2((tops[t] - top) * LOG2)
                total = total + sums[t] * w
                rdot = rdot + dots[t] * w
            mst[unit, half] = jnp.concatenate(tops[1:], axis=0)
            st_loc[unit, 0:3] = jnp.concatenate([top, total, rdot], axis=0)

        cell()

        @pl.when(half == 1)
        def _():
            s = st_loc[unit]
            st_all[unit, me8] = jnp.concatenate([tall(s[0:1]), tall(s[1:2]), tall(s[2:3]), jnp.zeros((1, HD), F32)], axis=0)
            repeat(1, 8, lambda k: st_copy(unit, k).start())

        return carry

    def drain_a():
        for r in range(4):
            all15(r).wait_send()
        for r in (1, 2, 3):
            for j in range(4):
                z_copy(r, j).wait_send()
        for i in range(2):
            kv_copy(i, kv.at[2, i], 2, zp).wait_send()
            kv_copy(i, kv.at[1, i], 1, sib).wait_send()
            kv_copy(i, kv.at[3, i], 3, sib).wait_send()
        repeat(0, 4, lambda u: st_seven(u).wait_send())

    lax.fori_loop(0, 8, phase1, 0)

    def combine(unit):
        st_seven(unit).wait_recv()
        stats = st_all[unit]
        top = jnp.max(stats[:, 0:SHARE], axis=0)
        w = jnp.exp2((stats[:, 0:SHARE] - top[None]) * LOG2)
        total = jnp.sum(stats[:, SHARE : 2 * SHARE] * w, axis=0)
        rdot = jnp.sum(stats[:, 2 * SHARE : 3 * SHARE] * w, axis=0) / total
        top, inv = wide(top), wide(1.0 / total)
        rdots[unit] = wide(rdot)
        mst[unit] = jnp.exp2((mst[unit] - top[None]) * LOG2) * inv[None]


    c_copy = [remote(c_out.at[n], c_in.at[n], c_sem.at[0, n], c_sem.at[1, n], sib) for n in range(2)]
    zz_copy = [remote(zz_out.at[i], zz_in.at[i], zz_sem.at[0, i], zz_sem.at[1, i], zp) for i in range(2)]

    def r_copy(r, k):
        dest = (x + k) % 4
        return remote(r_out.at[r, dest], r_in.at[r, x], r_send.at[r], r_recv.at[r], at_x(k))

    def r_three(r):
        part = r_in.at[r, pl.ds(0, 3)]
        return remote(part, part, r_send.at[r], r_recv.at[r], at_x(1))

    def scatter(r):
        dq = dq_acc[source(r)]
        for n in range(4):
            r_out[r, n] = dq[n * 4 * BLK : (n + 1) * 4 * BLK].astype(BF16)
        for k in (1, 2, 3):
            r_copy(r, k).start()

    def f_copy(r, k):
        head = (y + k) % 4
        return remote(f_out.at[r, head], f_in.at[me16], f_send.at[r], f_recv.at[r], place(order[r] * 4 + head))

    def f_part(r):
        count = 3 if r == 0 else 4
        part = f_in.at[pl.ds(0, count)]
        return remote(part, part, f_send.at[r], f_recv.at[r], place(order[r] * 4 + y))

    keep = pltpu.make_async_copy(f_out.at[0, y], f_in.at[me16], loc_sem.at[0])

    def deliver(r):
        r_three(r).wait_recv()
        tot = dq_acc[order[r], pl.ds(pl.multiple_of(x * 4 * BLK, 4 * BLK), 4 * BLK)]
        for k in (1, 2, 3):
            tot = tot + r_in[r, (x + k) % 4].astype(F32)
        pad = jnp.zeros((8, HD), F32)
        for n in range(4):
            f_out[r, n] = jnp.concatenate([tot[n * BLK : (n + 1) * BLK], pad], axis=0).astype(BF16)
        if r == 0:
            keep.start()
        repeat(1 if r == 0 else 0, 4, lambda k: f_copy(r, k).start())

    def c_start(n):
        rows = pl.ds((1 + 2 * n) * SPAN, SPAN)
        c_out[n, 0] = (dka[rows] * SCALE).astype(BF16)
        c_out[n, 1] = dva[rows].astype(BF16)
        c_copy[n].start()

    def q_step(n):
        r = n + 1 - 2 * (n % 2)
        unit = source(r)
        combine(unit)
        rdot = rdots[unit]
        dq_t = jnp.zeros((HD, UNIT), F32)
        for t in range(NT):
            rows = pl.ds(t * KT, KT)
            p = e_buf[unit, rows] * mst[unit, t // 4, t % 4 : t % 4 + 1]
            ds = p * (dp_buf[unit, rows] - rdot)
            dp_buf[unit, rows] = ds
            dq_t += dot(k_t[t // 4, :, t % 4 * KT : (t % 4 + 1) * KT], ds.astype(BF16))
        dq_acc[unit] = dq_t.T * SCALE
        scatter(r)

    def kv_step(unit, half):
        qu, dou, factor = q_s[unit], do_s[unit], mst[unit, half]
        for t in range(NT // 2):
            rows = pl.ds(half * 2 * SPAN + t * KT, KT)
            p = (e_buf[unit, rows] * factor[t : t + 1]).astype(BF16)
            dva[rows] += dot(p, dou)
            dka[rows] += dot(dp_buf[unit, rows].astype(BF16), qu)

    repeat(0, 2, q_step)
    repeat(0, 2, lambda n: kv_step(source(n), 1))
    repeat(2, 4, q_step)
    repeat(2, 4, lambda n: kv_step(source(n), 1))
    c_start(1)
    deliver(1)
    deliver(0)

    def near_step(n):
        kv_step(source(n), 0)

        @pl.when(n == 0)
        def _():
            c_copy[1].wait_recv()
            far = pl.ds(2 * SPAN, SPAN)
            zz_out[0] = (dka[far] * SCALE + c_in[1, 0].astype(F32)).astype(BF16)
            zz_out[1] = (dva[far] + c_in[1, 1].astype(F32)).astype(BF16)

        @pl.when(n == 1)
        def _():
            deliver(3)
            zz_copy[0].start()

        @pl.when(n == 2)
        def _():
            deliver(2)
            zz_copy[1].start()

    repeat(0, 4, near_step)
    c_start(0)

    c_copy[0].wait_recv()
    near = pl.ds(0, SPAN)
    dka[near] = dka[near] * SCALE + c_in[0, 0].astype(F32)
    dva[near] = dva[near] + c_in[0, 1].astype(F32)
    stores = []
    for i, (near_sum, out) in enumerate(((dka, dk_hbm), (dva, dv_hbm))):
        zz_copy[i].wait_recv()
        done[i] = (near_sum[near] + zz_in[i].astype(F32)).astype(BF16)
        stores.append(pltpu.make_async_copy(done.at[i], out, loc_sem.at[1 + i]))
        stores[i].start()

    for r in range(4):
        f_part(r).wait_recv()

    keep.wait()
    for store in stores:
        store.wait()
    drain_a()
    for n in range(2):
        c_copy[n].wait_send()
    for i in range(2):
        zz_copy[i].wait_send()
    for r in range(4):
        r_three(r).wait_send()
        f_part(r).wait_send()


def assemble(f_ref, dk_in, dv_in, dq_ref, dk_ref, dv_ref):
    out = []
    for b in range(KH):
        first = (b % 2) * 8 + b // 2
        blk = f_ref[first].astype(F32) + f_ref[first + 4].astype(F32)
        out += [blk[a * OWN : (a + 1) * OWN] for a in range(SHARE)]
    dq_ref[...] = jnp.concatenate(out, axis=1).astype(BF16)
    dk_ref[...] = dk_in[...]
    dv_ref[...] = dv_in[...]


def on_device(queries, grad_out, keys, values, prompt_len, resp_len):
    vmem = pl.BlockSpec(memory_space=pltpu.VMEM)
    smem = pl.BlockSpec(memory_space=pltpu.SMEM)
    hbm = pl.BlockSpec(memory_space=pl.ANY)
    dma = pltpu.SemaphoreType.DMA
    parts = pl.pallas_call(
        kernel,
        out_shape=[
            jax.ShapeDtypeStruct((16, BLK + 8, HD), BF16),
            jax.ShapeDtypeStruct((SPAN, HD), BF16),
            jax.ShapeDtypeStruct((SPAN, HD), BF16),
        ],
        in_specs=[smem, smem, hbm, hbm, hbm, hbm],
        out_specs=[hbm, hbm, hbm],
        scratch_shapes=[
            pltpu.VMEM((OWN, QH * HD), BF16),
            pltpu.VMEM((OWN, QH * HD), BF16),
            pltpu.VMEM((2, 4, 2 * BLK, HD), BF16),
            pltpu.VMEM((4, 4, 2 * BLK, HD), BF16),
            pltpu.VMEM((4, 16, 2 * BLK, HD), BF16),
            pltpu.VMEM((4, UNIT, HD), BF16),
            pltpu.VMEM((4, UNIT, HD), BF16),
            pltpu.VMEM((4, 2, SPAN, HD), BF16),
            pltpu.VMEM((2, HD, 2 * SPAN), BF16),
            pltpu.VMEM((4, KEYS, UNIT), F32),
            pltpu.VMEM((4, KEYS, UNIT), F32),
            pltpu.VMEM((4, 2, NT // 2, UNIT), F32),
            pltpu.VMEM((4, 8, UNIT), F32),
            pltpu.VMEM((4, 8, 16, HD), F32),
            pltpu.VMEM((4, 1, UNIT), F32),
            pltpu.VMEM((KEYS, HD), F32),
            pltpu.VMEM((KEYS, HD), F32),
            pltpu.VMEM((4, UNIT, HD), F32),
            pltpu.VMEM((4, 4, 4 * BLK, HD), BF16),
            pltpu.VMEM((4, 4, 4 * BLK, HD), BF16),
            pltpu.VMEM((4, 4, BLK + 8, HD), BF16),
            pltpu.VMEM((2, 2, SPAN, HD), BF16),
            pltpu.VMEM((2, 2, SPAN, HD), BF16),
            pltpu.VMEM((2, SPAN, HD), BF16),
            pltpu.VMEM((2, SPAN, HD), BF16),
            pltpu.VMEM((2, SPAN, HD), BF16),
            dma((4,)),
            dma((4, 2)),
            dma((4, 2)),
            dma((4, 4)),
            dma((4, 4)),
            dma((4,)),
            dma((4,)),
            dma((4,)),
            dma((4,)),
            dma((4,)),
            dma((4,)),
            dma((4,)),
            dma((4,)),
            dma((2, 2)),
            dma((2, 2)),
        ],
        compiler_params=pltpu.CompilerParams(
            collective_id=0, has_side_effects=True, vmem_limit_bytes=60 * 2**20
        ),
        name="window_grads",
    )(prompt_len, resp_len, queries, grad_out, keys, values)
    return pl.pallas_call(
        assemble,
        out_shape=[
            jax.ShapeDtypeStruct((OWN, QH * HD), BF16),
            jax.ShapeDtypeStruct((SPAN, HD), BF16),
            jax.ShapeDtypeStruct((SPAN, HD), BF16),
        ],
        in_specs=[vmem] * 3,
        out_specs=[vmem] * 3,
        name="assemble",
    )(*parts)


def solution(mesh):
    in_specs = (
        P(("group", "ctx"), None),
        P(("group", "ctx"), None),
        P("ctx", None),
        P("ctx", None),
        P(),
        P("group", None),
    )
    out_specs = (P(("group", "ctx"), None), P("ctx", "group"), P("ctx", "group"))
    return jax.shard_map(
        on_device, mesh=mesh, in_specs=in_specs, out_specs=out_specs, check_vma=False
    )
```

```python
import functools
import math

import jax
import jax.numpy as jnp
from jax import lax
from jax.experimental import pallas as pl
from jax.experimental.pallas import tpu as pltpu
from jax.sharding import PartitionSpec as P

QH = 40
KH = 8
HD = 128
SHARE = QH // KH
WINDOW = 128
SPAN = 512
OWN = 8
BLK = OWN * SHARE
UNIT = 16 * BLK
KT = 256
KEYS = 4 * SPAN
NT = KEYS // KT
SCALE = 1.0 / math.sqrt(HD)
LOG2 = SCALE * math.log2(math.e)
TRANS = (((1,), (1,)), ((), ()))
MESH = pl.DeviceIdType.MESH
F32 = jnp.float32
BF16 = jnp.bfloat16


def dot(a, b):
    return jnp.dot(a, b, preferred_element_type=F32)


def dot_t(a, b):
    return lax.dot_general(a, b, TRANS, preferred_element_type=F32)


def wide(rows):
    return jnp.concatenate([rows[i : i + 1] for i in range(SHARE)], axis=1)


def tall(row):
    return jnp.concatenate([row[:, i * HD : (i + 1) * HD] for i in range(SHARE)], axis=0)


def kernel(
    plen_ref, rlen_ref, q_hbm, do_hbm, k_hbm, v_hbm,
    f_in, dk_hbm, dv_hbm,
    q_ref, do_ref, snd, held, gath, q_s, do_s, kv, k_t, e_buf, dp_buf, mst, st_loc, st_all, rdots, dka, dva, dq_acc,
    r_out, r_in, f_out, c_out, c_in, zz_out, zz_in, done,
    loc_sem, kv_send, kv_recv, z_send, z_recv, g_send, g_recv, st_send, st_recv,
    r_send, r_recv, f_send, f_recv, c_sem, zz_sem,
):
    g = lax.axis_index("group")
    c = lax.axis_index("ctx")
    core = c % 2
    z_lo = (c // 2) % 4
    x = c // 8
    par = z_lo % 2
    zl = z_lo // 2
    y = g // 2
    z_hi = g % 2
    zq = z_hi * 2 + zl
    pq = z_hi * 2 + 1 - zl
    order = [zq, pq, 3 - zq, 3 - pq]
    me16 = zq * 4 + y
    me8 = x * 2 + zl

    def ctx_of(x_, z_lo_, core_):
        return (x_ * 4 + z_lo_) * 2 + core_

    sib = (g, ctx_of(x, z_lo, 1 - core))
    zp_lo = z_lo + 1 - 2 * par
    zp = (g, ctx_of(x, zp_lo, core))
    mate = (g, ctx_of(x, (1 - zl) * 2 + par, core))

    def place(dest):
        z_ = dest // 4
        return ((dest % 4) * 2 + z_ // 2, ctx_of(x, (z_ % 2) * 2 + par, core))

    def ring(k):
        dest = (me8 + k) % 8
        return (g, ctx_of(dest // 2, (dest % 2) * 2 + par, core))

    def at_x(k):
        return (g, ctx_of((x + k) % 4, z_lo, core))

    def remote(src, dst, send, recv, dev):
        return pltpu.make_async_remote_copy(
            src_ref=src, dst_ref=dst, send_sem=send, recv_sem=recv, device_id=dev, device_id_type=MESH
        )

    def repeat(first, last, step):
        def body(k, s):
            step(k)
            return s

        lax.fori_loop(first, last, body, 0)

    def level(k):
        return (((y + k) % 4) * 2 + z_hi, ctx_of((x + k // 4) % 4, z_lo, core))

    loads = [pltpu.make_async_copy(a, b, loc_sem.at[2 + i]) for i, (a, b) in enumerate(((q_hbm, q_ref), (do_hbm, do_ref)))]
    for cp in loads:
        cp.start()

    barrier = pltpu.get_barrier_semaphore()

    def greet(dev):
        pl.semaphore_signal(barrier, inc=1, device_id=dev, device_id_type=MESH)

    repeat(1, 16, lambda k: greet(level(k)))
    repeat(0, 12, lambda k: greet(place((zq * 4 + 4 + k) % 16)))
    for dx in (1, 2, 3):
        greet((g, ctx_of((x + dx) % 4, (1 - zl) * 2 + par, core)))
    greet(sib)
    greet(zp)

    cols = pl.ds(pl.multiple_of(g * HD, HD), HD)
    local = [
        pltpu.make_async_copy(h.at[:, cols], kv.at[0, i], loc_sem.at[i]) for i, h in enumerate((k_hbm, v_hbm))
    ]
    for cp in local:
        cp.start()

    for cp in loads:
        cp.wait()
    qf = q_ref[...].astype(F32)
    live_to = rlen_ref[0, c // 16]
    t_row = (c % 16) * OWN + lax.broadcasted_iota(jnp.int32, (OWN, 1), 0)
    dof = jnp.where(t_row < live_to, do_ref[...].astype(F32), 0.0)
    for b in range(KH):
        rows = [m[:, (b * SHARE + a) * HD : (b * SHARE + a + 1) * HD] for m in (qf, dof) for a in range(SHARE)]
        snd[b % 2, b // 2] = jnp.concatenate(rows, axis=0).astype(BF16)
    gath[zq, x * 4 + y] = snd[z_hi, y]

    pl.semaphore_wait(barrier, 32)

    def z_copy(r, j):
        head = (y + j) % 4
        if r == 3:
            part = held.at[order[2], head]
            return remote(part, part, z_send.at[3, head], z_recv.at[3, head], mate)
        half = z_hi if r == 1 else 1 - z_hi
        dev = place(order[r] * 4 + y)
        return remote(snd.at[half, head], held.at[zq, head], z_send.at[r, head], z_recv.at[r, head], dev)

    def g_copy(r, j, dx):
        zr = order[r]
        head = (y + j) % 4
        src = snd.at[z_hi, head] if r == 0 else held.at[zr, head]
        return remote(src, gath.at[zr, x * 4 + y], g_send.at[r], g_recv.at[r], level(dx * 4 + j))

    def spread(r):
        for j in range(4):
            if r > 0:
                z_copy(r, j).wait_recv()
            if r == 2:
                z_copy(3, j).start()
            if r > 0 and j == 0:
                gath[order[r], x * 4 + y] = held[order[r], y]
            repeat(1 if j == 0 else 0, 4, lambda dx: g_copy(r, j, dx).start())

    def all15(r):
        part = gath.at[order[r], pl.ds(0, 15)]
        return remote(part, part, g_send.at[r], g_recv.at[r], level(1))

    for j in range(4):
        z_copy(1, j).start()
    for j in range(4):
        z_copy(2, j).start()
    spread(0)

    def kv_copy(i, src, slot, dev):
        return remote(src, kv.at[slot, i], kv_send.at[slot, i], kv_recv.at[slot, i], dev)

    for i, h in enumerate((k_hbm, v_hbm)):
        kv_copy(i, h.at[:, cols], 1, sib).start()
        kv_copy(i, h.at[:, cols], 2, zp).start()

    dka[...] = jnp.zeros_like(dka)
    dva[...] = jnp.zeros_like(dva)
    st_loc[...] = jnp.concatenate([jnp.full((4, 1, UNIT), -1e30, F32), jnp.zeros((4, 7, UNIT), F32)], axis=1)

    spread(1)
    spread(2)
    for cp in local:
        cp.wait()
    for i in range(2):
        kv_copy(i, kv.at[1, i], 1, sib).wait_recv()

    def turn(slot):
        k_t[slot // 2, :, slot % 2 * SPAN : (slot % 2 + 1) * SPAN] = kv[slot, 0].astype(F32).T.astype(BF16)

    turn(0)
    turn(1)
    plen = plen_ref[0]
    c_zp = zp[1]
    c_base = [c * SPAN, sib[1] * SPAN, c_zp * SPAN, (c_zp + 1 - 2 * core) * SPAN]

    def st_copy(unit, k):
        return remote(
            st_all.at[unit, me8], st_all.at[unit, me8], st_send.at[unit], st_recv.at[unit], ring(k)
        )

    def st_seven(unit):
        part = st_all.at[unit, pl.ds(0, 7)]
        return remote(part, part, st_send.at[unit], st_recv.at[unit], ring(1))

    def source(r):
        same = (1 - r // 2) * z_hi + (r // 2) * (1 - z_hi)
        mine = (1 - r % 2) * zl + (r % 2) * (1 - zl)
        return same * 2 + (1 - r // 2) * mine + (r // 2) * (1 - mine)

    def phase1(i, carry):
        unit, half = source(i // 2), i % 2

        @pl.when(i == 0)
        def _():
            all15(0).wait_recv()

        @pl.when(i == 1)
        def _():
            for i_ in range(2):
                kv_copy(i_, kv.at[2, i_], 2, zp).wait_recv()
                kv_copy(i_, kv.at[2, i_], 3, sib).start()
            spread(3)
            turn(2)
            for i_ in range(2):
                kv_copy(i_, kv.at[3, i_], 3, sib).wait_recv()
            turn(3)

        @pl.when(i == 2)
        def _():
            all15(1).wait_recv()

        @pl.when(i == 4)
        def _():
            all15(2).wait_recv()

        @pl.when(i == 6)
        def _():
            all15(3).wait_recv()

        @pl.when(half == 0)
        def _():
            both = gath[unit].astype(F32)
            q_s[unit] = both[:, :BLK].reshape(UNIT, HD).astype(BF16)
            do_s[unit] = both[:, BLK:].reshape(UNIT, HD).astype(BF16)

        def cell():
            qu, dou = q_s[unit], do_s[unit]
            old = st_loc[unit]
            tops, sums, dots = [old[0:1]], [old[1:2]], [old[2:3]]
            for t in range(NT // 2):
                slot, part = half * 2 + t // 2, pl.ds(t % 2 * KT, KT)
                rows = pl.ds(pl.multiple_of(half * 2 * SPAN + t * KT, KT), KT)
                s = dot_t(kv[slot, 0, part], qu)
                if t % 2 == 1:
                    base = jnp.where(half == 0, c_base[t // 2], c_base[2 + t // 2]) + KT
                    at = base + lax.broadcasted_iota(jnp.int32, (KT, 1), 0)
                    s = jnp.where(at < plen, s, -1e30)
                dp = dot_t(kv[slot, 1, part], dou)
                top = jnp.max(s, axis=0, keepdims=True)
                e = jnp.exp2((s - top) * LOG2)
                e_buf[unit, rows] = e
                dp_buf[unit, rows] = dp
                tops.append(top)
                sums.append(jnp.sum(e, axis=0, keepdims=True))
                dots.append(jnp.sum(e * dp, axis=0, keepdims=True))
            top = functools.reduce(jnp.maximum, tops)
            total, rdot = 0.0, 0.0
            for t in range(NT // 2 + 1):
                w = jnp.exp2((tops[t] - top) * LOG2)
                total = total + sums[t] * w
                rdot = rdot + dots[t] * w
            mst[unit, half] = jnp.concatenate(tops[1:], axis=0)
            st_loc[unit, 0:3] = jnp.concatenate([top, total, rdot], axis=0)

        cell()

        @pl.when(half == 1)
        def _():
            s = st_loc[unit]
            st_all[unit, me8] = jnp.concatenate([tall(s[0:1]), tall(s[1:2]), tall(s[2:3]), jnp.zeros((1, HD), F32)], axis=0)
            repeat(1, 8, lambda k: st_copy(unit, k).start())

        return carry

    def drain_a():
        for r in range(4):
            all15(r).wait_send()
        for r in (1, 2, 3):
            for j in range(4):
                z_copy(r, j).wait_send()
        for i in range(2):
            kv_copy(i, kv.at[2, i], 2, zp).wait_send()
            kv_copy(i, kv.at[1, i], 1, sib).wait_send()
            kv_copy(i, kv.at[3, i], 3, sib).wait_send()
        repeat(0, 4, lambda u: st_seven(u).wait_send())

    lax.fori_loop(0, 8, phase1, 0)

    def combine(unit):
        st_seven(unit).wait_recv()
        stats = st_all[unit]
        top = jnp.max(stats[:, 0:SHARE], axis=0)
        w = jnp.exp2((stats[:, 0:SHARE] - top[None]) * LOG2)
        total = jnp.sum(stats[:, SHARE : 2 * SHARE] * w, axis=0)
        rdot = jnp.sum(stats[:, 2 * SHARE : 3 * SHARE] * w, axis=0) / total
        top, inv = wide(top), wide(1.0 / total)
        rdots[unit] = wide(rdot)
        mst[unit] = jnp.exp2((mst[unit] - top[None]) * LOG2) * inv[None]


    c_copy = [
        [remote(c_out.at[n, i], c_in.at[n, i], c_sem.at[0, n, i], c_sem.at[1, n, i], sib) for i in range(2)]
        for n in range(2)
    ]
    zz_copy = [remote(zz_out.at[i], zz_in.at[i], zz_sem.at[0, i], zz_sem.at[1, i], zp) for i in range(2)]

    def r_copy(r, k):
        dest = (x + k) % 4
        return remote(r_out.at[r, dest], r_in.at[r, x], r_send.at[r], r_recv.at[r], at_x(k))

    def r_three(r):
        part = r_in.at[r, pl.ds(0, 3)]
        return remote(part, part, r_send.at[r], r_recv.at[r], at_x(1))

    def scatter(r):
        dq = dq_acc[source(r)]
        for n in range(4):
            r_out[r, n] = dq[n * 4 * BLK : (n + 1) * 4 * BLK].astype(BF16)
        for k in (1, 2, 3):
            r_copy(r, k).start()

    def f_copy(r, k):
        head = (y + k) % 4
        return remote(f_out.at[r, head], f_in.at[me16], f_send.at[r], f_recv.at[r], place(order[r] * 4 + head))

    def f_part(r):
        count = 3 if r == 0 else 4
        part = f_in.at[pl.ds(0, count)]
        return remote(part, part, f_send.at[r], f_recv.at[r], place(order[r] * 4 + y))

    keep = pltpu.make_async_copy(f_out.at[0, y], f_in.at[me16], loc_sem.at[0])

    def deliver(r):
        r_three(r).wait_recv()
        tot = dq_acc[order[r], pl.ds(pl.multiple_of(x * 4 * BLK, 4 * BLK), 4 * BLK)]
        for k in (1, 2, 3):
            tot = tot + r_in[r, (x + k) % 4].astype(F32)
        pad = jnp.zeros((8, HD), F32)
        for n in range(4):
            f_out[r, n] = jnp.concatenate([tot[n * BLK : (n + 1) * BLK], pad], axis=0).astype(BF16)
        if r == 0:
            keep.start()
        repeat(1 if r == 0 else 0, 4, lambda k: f_copy(r, k).start())

    def c_start(n, i):
        rows = pl.ds((1 + 2 * n) * SPAN, SPAN)
        c_out[n, i] = (dka[rows] * SCALE if i == 0 else dva[rows]).astype(BF16)
        c_copy[n][i].start()

    def zz_make(i):
        c_copy[1][i].wait_recv()
        far = pl.ds(2 * SPAN, SPAN)
        mine = dka[far] * SCALE if i == 0 else dva[far]
        zz_out[i] = (mine + c_in[1, i].astype(F32)).astype(BF16)

    def q_step(n):
        r = n + 1 - 2 * (n % 2)
        unit = source(r)
        combine(unit)
        rdot = rdots[unit]
        dq_t = jnp.zeros((HD, UNIT), F32)
        for t in range(NT):
            rows = pl.ds(t * KT, KT)
            p = e_buf[unit, rows] * mst[unit, t // 4, t % 4 : t % 4 + 1]
            ds = p * (dp_buf[unit, rows] - rdot)
            dp_buf[unit, rows] = ds
            dq_t += dot(k_t[t // 4, :, t % 4 * KT : (t % 4 + 1) * KT], ds.astype(BF16))
        dq_acc[unit] = dq_t.T * SCALE
        scatter(r)

    def kv_step(unit, half, key=True, value=True):
        qu, dou, factor = q_s[unit], do_s[unit], mst[unit, half]
        for t in range(NT // 2):
            rows = pl.ds(half * 2 * SPAN + t * KT, KT)
            if value:
                dva[rows] += dot((e_buf[unit, rows] * factor[t : t + 1]).astype(BF16), dou)
            if key:
                dka[rows] += dot(dp_buf[unit, rows].astype(BF16), qu)

    repeat(0, 2, q_step)
    repeat(0, 2, lambda n: kv_step(source(n), 1))
    repeat(2, 4, q_step)
    repeat(2, 4, lambda n: kv_step(source(n), 1, key=False))
    c_start(1, 1)
    repeat(2, 4, lambda n: kv_step(source(n), 1, value=False))
    c_start(1, 0)
    deliver(1)
    deliver(0)
    zz_make(1)
    zz_copy[1].start()

    def near_step(n):
        kv_step(source(n), 0)

        @pl.when(n == 0)
        def _():
            zz_make(0)
            deliver(3)

        @pl.when(n == 2)
        def _():
            deliver(2)
            zz_copy[0].start()

    repeat(0, 4, near_step)
    c_start(0, 0)
    c_start(0, 1)

    for i in range(2):
        c_copy[0][i].wait_recv()
    near = pl.ds(0, SPAN)
    dka[near] = dka[near] * SCALE + c_in[0, 0].astype(F32)
    dva[near] = dva[near] + c_in[0, 1].astype(F32)
    stores = []
    for i, (near_sum, out) in enumerate(((dka, dk_hbm), (dva, dv_hbm))):
        zz_copy[i].wait_recv()
        done[i] = (near_sum[near] + zz_in[i].astype(F32)).astype(BF16)
        stores.append(pltpu.make_async_copy(done.at[i], out, loc_sem.at[1 + i]))
        stores[i].start()

    for r in range(4):
        f_part(r).wait_recv()

    keep.wait()
    for store in stores:
        store.wait()
    drain_a()
    for n in range(2):
        for i in range(2):
            c_copy[n][i].wait_send()
    for i in range(2):
        zz_copy[i].wait_send()
    for r in range(4):
        r_three(r).wait_send()
        f_part(r).wait_send()


def assemble(f_ref, dk_in, dv_in, dq_ref, dk_ref, dv_ref):
    out = []
    for b in range(KH):
        first = (b % 2) * 8 + b // 2
        blk = f_ref[first].astype(F32) + f_ref[first + 4].astype(F32)
        out += [blk[a * OWN : (a + 1) * OWN] for a in range(SHARE)]
    dq_ref[...] = jnp.concatenate(out, axis=1).astype(BF16)
    dk_ref[...] = dk_in[...]
    dv_ref[...] = dv_in[...]


def on_device(queries, grad_out, keys, values, prompt_len, resp_len):
    vmem = pl.BlockSpec(memory_space=pltpu.VMEM)
    smem = pl.BlockSpec(memory_space=pltpu.SMEM)
    hbm = pl.BlockSpec(memory_space=pl.ANY)
    dma = pltpu.SemaphoreType.DMA
    parts = pl.pallas_call(
        kernel,
        out_shape=[
            jax.ShapeDtypeStruct((16, BLK + 8, HD), BF16),
            jax.ShapeDtypeStruct((SPAN, HD), BF16),
            jax.ShapeDtypeStruct((SPAN, HD), BF16),
        ],
        in_specs=[smem, smem, hbm, hbm, hbm, hbm],
        out_specs=[hbm, hbm, hbm],
        scratch_shapes=[
            pltpu.VMEM((OWN, QH * HD), BF16),
            pltpu.VMEM((OWN, QH * HD), BF16),
            pltpu.VMEM((2, 4, 2 * BLK, HD), BF16),
            pltpu.VMEM((4, 4, 2 * BLK, HD), BF16),
            pltpu.VMEM((4, 16, 2 * BLK, HD), BF16),
            pltpu.VMEM((4, UNIT, HD), BF16),
            pltpu.VMEM((4, UNIT, HD), BF16),
            pltpu.VMEM((4, 2, SPAN, HD), BF16),
            pltpu.VMEM((2, HD, 2 * SPAN), BF16),
            pltpu.VMEM((4, KEYS, UNIT), F32),
            pltpu.VMEM((4, KEYS, UNIT), F32),
            pltpu.VMEM((4, 2, NT // 2, UNIT), F32),
            pltpu.VMEM((4, 8, UNIT), F32),
            pltpu.VMEM((4, 8, 16, HD), F32),
            pltpu.VMEM((4, 1, UNIT), F32),
            pltpu.VMEM((KEYS, HD), F32),
            pltpu.VMEM((KEYS, HD), F32),
            pltpu.VMEM((4, UNIT, HD), F32),
            pltpu.VMEM((4, 4, 4 * BLK, HD), BF16),
            pltpu.VMEM((4, 4, 4 * BLK, HD), BF16),
            pltpu.VMEM((4, 4, BLK + 8, HD), BF16),
            pltpu.VMEM((2, 2, SPAN, HD), BF16),
            pltpu.VMEM((2, 2, SPAN, HD), BF16),
            pltpu.VMEM((2, SPAN, HD), BF16),
            pltpu.VMEM((2, SPAN, HD), BF16),
            pltpu.VMEM((2, SPAN, HD), BF16),
            dma((4,)),
            dma((4, 2)),
            dma((4, 2)),
            dma((4, 4)),
            dma((4, 4)),
            dma((4,)),
            dma((4,)),
            dma((4,)),
            dma((4,)),
            dma((4,)),
            dma((4,)),
            dma((4,)),
            dma((4,)),
            dma((2, 2, 2)),
            dma((2, 2)),
        ],
        compiler_params=pltpu.CompilerParams(
            collective_id=0, has_side_effects=True, vmem_limit_bytes=60 * 2**20
        ),
        name="window_grads",
    )(prompt_len, resp_len, queries, grad_out, keys, values)
    return pl.pallas_call(
        assemble,
        out_shape=[
            jax.ShapeDtypeStruct((OWN, QH * HD), BF16),
            jax.ShapeDtypeStruct((SPAN, HD), BF16),
            jax.ShapeDtypeStruct((SPAN, HD), BF16),
        ],
        in_specs=[vmem] * 3,
        out_specs=[vmem] * 3,
        name="assemble",
    )(*parts)


def solution(mesh):
    in_specs = (
        P(("group", "ctx"), None),
        P(("group", "ctx"), None),
        P("ctx", None),
        P("ctx", None),
        P(),
        P("group", None),
    )
    out_specs = (P(("group", "ctx"), None), P("ctx", "group"), P("ctx", "group"))
    return jax.shard_map(
        on_device, mesh=mesh, in_specs=in_specs, out_specs=out_specs, check_vma=False
    )
```

```python
import functools
import math

import jax
import jax.numpy as jnp
from jax import lax
from jax.experimental import pallas as pl
from jax.experimental.pallas import tpu as pltpu
from jax.sharding import PartitionSpec as P

QH = 40
KH = 8
HD = 128
SHARE = QH // KH
WINDOW = 128
SPAN = 512
OWN = 8
BLK = OWN * SHARE
UNIT = 16 * BLK
KT = 256
KEYS = 4 * SPAN
NT = KEYS // KT
SCALE = 1.0 / math.sqrt(HD)
LOG2 = SCALE * math.log2(math.e)
TRANS = (((1,), (1,)), ((), ()))
MESH = pl.DeviceIdType.MESH
F32 = jnp.float32
BF16 = jnp.bfloat16


def dot(a, b):
    return jnp.dot(a, b, preferred_element_type=F32)


def dot_t(a, b):
    return lax.dot_general(a, b, TRANS, preferred_element_type=F32)


def wide(rows):
    return jnp.concatenate([rows[i : i + 1] for i in range(SHARE)], axis=1)


def tall(row):
    return jnp.concatenate([row[:, i * HD : (i + 1) * HD] for i in range(SHARE)], axis=0)


def kernel(
    plen_ref, rlen_ref, q_hbm, do_hbm, k_hbm, v_hbm,
    f_in, dk_hbm, dv_hbm,
    q_ref, do_ref, snd, held, gath, q_s, do_s, kv, k_t, e_buf, dp_buf, mst, st_loc, st_all, rdots, dka, dva, dq_acc,
    r_out, r_in, f_out, c_out, c_in, zz_out, zz_in, done,
    loc_sem, kv_send, kv_recv, z_send, z_recv, g_send, g_recv, st_send, st_recv,
    r_send, r_recv, f_send, f_recv, c_sem, zz_sem,
):
    g = lax.axis_index("group")
    c = lax.axis_index("ctx")
    core = c % 2
    z_lo = (c // 2) % 4
    x = c // 8
    par = z_lo % 2
    zl = z_lo // 2
    y = g // 2
    z_hi = g % 2
    zq = z_hi * 2 + zl
    pq = z_hi * 2 + 1 - zl
    order = [zq, pq, 3 - zq, 3 - pq]
    me16 = zq * 4 + y
    me8 = x * 2 + zl

    def ctx_of(x_, z_lo_, core_):
        return (x_ * 4 + z_lo_) * 2 + core_

    sib = (g, ctx_of(x, z_lo, 1 - core))
    zp_lo = z_lo + 1 - 2 * par
    zp = (g, ctx_of(x, zp_lo, core))
    mate = (g, ctx_of(x, (1 - zl) * 2 + par, core))

    def place(dest):
        z_ = dest // 4
        return ((dest % 4) * 2 + z_ // 2, ctx_of(x, (z_ % 2) * 2 + par, core))

    def ring(k):
        dest = (me8 + k) % 8
        return (g, ctx_of(dest // 2, (dest % 2) * 2 + par, core))

    def at_x(k):
        return (g, ctx_of((x + k) % 4, z_lo, core))

    def remote(src, dst, send, recv, dev):
        return pltpu.make_async_remote_copy(
            src_ref=src, dst_ref=dst, send_sem=send, recv_sem=recv, device_id=dev, device_id_type=MESH
        )

    def repeat(first, last, step):
        def body(k, s):
            step(k)
            return s

        lax.fori_loop(first, last, body, 0)

    def level(k):
        return (((y + k) % 4) * 2 + z_hi, ctx_of((x + k // 4) % 4, z_lo, core))

    loads = [pltpu.make_async_copy(a, b, loc_sem.at[2 + i]) for i, (a, b) in enumerate(((q_hbm, q_ref), (do_hbm, do_ref)))]
    for cp in loads:
        cp.start()

    barrier = pltpu.get_barrier_semaphore()

    def greet(dev):
        pl.semaphore_signal(barrier, inc=1, device_id=dev, device_id_type=MESH)

    repeat(1, 16, lambda k: greet(level(k)))
    repeat(0, 12, lambda k: greet(place((zq * 4 + 4 + k) % 16)))
    for dx in (1, 2, 3):
        greet((g, ctx_of((x + dx) % 4, (1 - zl) * 2 + par, core)))
    greet(sib)
    greet(zp)

    cols = pl.ds(pl.multiple_of(g * HD, HD), HD)
    local = [
        pltpu.make_async_copy(h.at[:, cols], kv.at[0, i], loc_sem.at[i]) for i, h in enumerate((k_hbm, v_hbm))
    ]
    for cp in local:
        cp.start()

    for cp in loads:
        cp.wait()
    qf = q_ref[...].astype(F32)
    live_to = rlen_ref[0, c // 16]
    t_row = (c % 16) * OWN + lax.broadcasted_iota(jnp.int32, (OWN, 1), 0)
    dof = jnp.where(t_row < live_to, do_ref[...].astype(F32), 0.0)
    for b in range(KH):
        rows = [m[:, (b * SHARE + a) * HD : (b * SHARE + a + 1) * HD] for m in (qf, dof) for a in range(SHARE)]
        snd[b % 2, b // 2] = jnp.concatenate(rows, axis=0).astype(BF16)
    gath[zq, x * 4 + y] = snd[z_hi, y]

    pl.semaphore_wait(barrier, 32)

    def z_copy(r, j):
        head = (y + j) % 4
        if r == 3:
            part = held.at[order[2], head]
            return remote(part, part, z_send.at[3, head], z_recv.at[3, head], mate)
        half = z_hi if r == 1 else 1 - z_hi
        dev = place(order[r] * 4 + y)
        return remote(snd.at[half, head], held.at[zq, head], z_send.at[r, head], z_recv.at[r, head], dev)

    def g_copy(r, j, dx):
        zr = order[r]
        head = (y + j) % 4
        src = snd.at[z_hi, head] if r == 0 else held.at[zr, head]
        return remote(src, gath.at[zr, x * 4 + y], g_send.at[r], g_recv.at[r], level(dx * 4 + j))

    def spread(r):
        for j in range(4):
            if r > 0:
                z_copy(r, j).wait_recv()
            if r == 2:
                z_copy(3, j).start()
            if r > 0 and j == 0:
                gath[order[r], x * 4 + y] = held[order[r], y]
            repeat(1 if j == 0 else 0, 4, lambda dx: g_copy(r, j, dx).start())

    def all15(r):
        part = gath.at[order[r], pl.ds(0, 15)]
        return remote(part, part, g_send.at[r], g_recv.at[r], level(1))

    for j in range(4):
        z_copy(2, j).start()
        z_copy(1, j).start()
    spread(0)

    def kv_copy(i, src, slot, dev):
        return remote(src, kv.at[slot, i], kv_send.at[slot, i], kv_recv.at[slot, i], dev)

    for i, h in enumerate((k_hbm, v_hbm)):
        kv_copy(i, h.at[:, cols], 1, sib).start()
        kv_copy(i, h.at[:, cols], 2, zp).start()

    dka[...] = jnp.zeros_like(dka)
    dva[...] = jnp.zeros_like(dva)
    st_loc[...] = jnp.concatenate([jnp.full((4, 1, UNIT), -1e30, F32), jnp.zeros((4, 7, UNIT), F32)], axis=1)

    spread(1)
    spread(2)
    for cp in local:
        cp.wait()
    for i in range(2):
        kv_copy(i, kv.at[1, i], 1, sib).wait_recv()

    def turn(slot):
        k_t[slot // 2, :, slot % 2 * SPAN : (slot % 2 + 1) * SPAN] = kv[slot, 0].astype(F32).T.astype(BF16)

    turn(0)
    turn(1)
    plen = plen_ref[0]
    c_zp = zp[1]
    c_base = [c * SPAN, sib[1] * SPAN, c_zp * SPAN, (c_zp + 1 - 2 * core) * SPAN]

    def st_copy(unit, k):
        return remote(
            st_all.at[unit, me8], st_all.at[unit, me8], st_send.at[unit], st_recv.at[unit], ring(k)
        )

    def st_seven(unit):
        part = st_all.at[unit, pl.ds(0, 7)]
        return remote(part, part, st_send.at[unit], st_recv.at[unit], ring(1))

    def source(r):
        same = (1 - r // 2) * z_hi + (r // 2) * (1 - z_hi)
        mine = (1 - r % 2) * zl + (r % 2) * (1 - zl)
        return same * 2 + (1 - r // 2) * mine + (r // 2) * (1 - mine)

    def phase1(i, carry):
        unit, half = source(i // 2), i % 2

        @pl.when(i == 0)
        def _():
            all15(0).wait_recv()

        @pl.when(i == 1)
        def _():
            for i_ in range(2):
                kv_copy(i_, kv.at[2, i_], 2, zp).wait_recv()
                kv_copy(i_, kv.at[2, i_], 3, sib).start()
            spread(3)
            turn(2)
            for i_ in range(2):
                kv_copy(i_, kv.at[3, i_], 3, sib).wait_recv()
            turn(3)

        @pl.when(i == 2)
        def _():
            all15(1).wait_recv()

        @pl.when(i == 4)
        def _():
            all15(2).wait_recv()

        @pl.when(i == 6)
        def _():
            all15(3).wait_recv()

        @pl.when(half == 0)
        def _():
            both = gath[unit].astype(F32)
            q_s[unit] = both[:, :BLK].reshape(UNIT, HD).astype(BF16)
            do_s[unit] = both[:, BLK:].reshape(UNIT, HD).astype(BF16)

        def cell():
            qu, dou = q_s[unit], do_s[unit]
            old = st_loc[unit]
            tops, sums, dots = [old[0:1]], [old[1:2]], [old[2:3]]
            for t in range(NT // 2):
                slot, part = half * 2 + t // 2, pl.ds(t % 2 * KT, KT)
                rows = pl.ds(pl.multiple_of(half * 2 * SPAN + t * KT, KT), KT)
                s = dot_t(kv[slot, 0, part], qu)
                if t % 2 == 1:
                    base = jnp.where(half == 0, c_base[t // 2], c_base[2 + t // 2]) + KT
                    at = base + lax.broadcasted_iota(jnp.int32, (KT, 1), 0)
                    s = jnp.where(at < plen, s, -1e30)
                dp = dot_t(kv[slot, 1, part], dou)
                top = jnp.max(s, axis=0, keepdims=True)
                e = jnp.exp2((s - top) * LOG2)
                e_buf[unit, rows] = e
                dp_buf[unit, rows] = dp
                tops.append(top)
                sums.append(jnp.sum(e, axis=0, keepdims=True))
                dots.append(jnp.sum(e * dp, axis=0, keepdims=True))
            top = functools.reduce(jnp.maximum, tops)
            total, rdot = 0.0, 0.0
            for t in range(NT // 2 + 1):
                w = jnp.exp2((tops[t] - top) * LOG2)
                total = total + sums[t] * w
                rdot = rdot + dots[t] * w
            mst[unit, half] = jnp.concatenate(tops[1:], axis=0)
            st_loc[unit, 0:3] = jnp.concatenate([top, total, rdot], axis=0)

        cell()

        @pl.when(half == 1)
        def _():
            s = st_loc[unit]
            st_all[unit, me8] = jnp.concatenate([tall(s[0:1]), tall(s[1:2]), tall(s[2:3]), jnp.zeros((1, HD), F32)], axis=0)
            repeat(1, 8, lambda k: st_copy(unit, k).start())

        return carry

    def drain_a():
        for r in range(4):
            all15(r).wait_send()
        for r in (1, 2, 3):
            for j in range(4):
                z_copy(r, j).wait_send()
        for i in range(2):
            kv_copy(i, kv.at[2, i], 2, zp).wait_send()
            kv_copy(i, kv.at[1, i], 1, sib).wait_send()
            kv_copy(i, kv.at[3, i], 3, sib).wait_send()
        repeat(0, 4, lambda u: st_seven(u).wait_send())

    lax.fori_loop(0, 8, phase1, 0)

    def combine(unit):
        st_seven(unit).wait_recv()
        stats = st_all[unit]
        top = jnp.max(stats[:, 0:SHARE], axis=0)
        w = jnp.exp2((stats[:, 0:SHARE] - top[None]) * LOG2)
        total = jnp.sum(stats[:, SHARE : 2 * SHARE] * w, axis=0)
        rdot = jnp.sum(stats[:, 2 * SHARE : 3 * SHARE] * w, axis=0) / total
        top, inv = wide(top), wide(1.0 / total)
        rdots[unit] = wide(rdot)
        mst[unit] = jnp.exp2((mst[unit] - top[None]) * LOG2) * inv[None]


    c_copy = [
        [remote(c_out.at[n, i], c_in.at[n, i], c_sem.at[0, n, i], c_sem.at[1, n, i], sib) for i in range(2)]
        for n in range(2)
    ]
    zz_copy = [remote(zz_out.at[i], zz_in.at[i], zz_sem.at[0, i], zz_sem.at[1, i], zp) for i in range(2)]

    def r_copy(r, k):
        dest = (x + k) % 4
        return remote(r_out.at[r, dest], r_in.at[r, x], r_send.at[r], r_recv.at[r], at_x(k))

    def r_three(r):
        part = r_in.at[r, pl.ds(0, 3)]
        return remote(part, part, r_send.at[r], r_recv.at[r], at_x(1))

    def scatter(r):
        dq = dq_acc[source(r)]
        for n in range(4):
            r_out[r, n] = dq[n * 4 * BLK : (n + 1) * 4 * BLK].astype(BF16)
        for k in (1, 2, 3):
            r_copy(r, k).start()

    def f_copy(r, k):
        head = (y + k) % 4
        return remote(f_out.at[r, head], f_in.at[me16], f_send.at[r], f_recv.at[r], place(order[r] * 4 + head))

    def f_part(r):
        count = 3 if r == 0 else 4
        part = f_in.at[pl.ds(0, count)]
        return remote(part, part, f_send.at[r], f_recv.at[r], place(order[r] * 4 + y))

    keep = pltpu.make_async_copy(f_out.at[0, y], f_in.at[me16], loc_sem.at[0])

    def deliver(r):
        r_three(r).wait_recv()
        tot = dq_acc[order[r], pl.ds(pl.multiple_of(x * 4 * BLK, 4 * BLK), 4 * BLK)]
        for k in (1, 2, 3):
            tot = tot + r_in[r, (x + k) % 4].astype(F32)
        pad = jnp.zeros((8, HD), F32)
        for n in range(4):
            f_out[r, n] = jnp.concatenate([tot[n * BLK : (n + 1) * BLK], pad], axis=0).astype(BF16)
        if r == 0:
            keep.start()
        repeat(1 if r == 0 else 0, 4, lambda k: f_copy(r, k).start())

    def c_start(n, i):
        rows = pl.ds((1 + 2 * n) * SPAN, SPAN)
        c_out[n, i] = (dka[rows] * SCALE if i == 0 else dva[rows]).astype(BF16)
        c_copy[n][i].start()

    def zz_make(i):
        c_copy[1][i].wait_recv()
        far = pl.ds(2 * SPAN, SPAN)
        mine = dka[far] * SCALE if i == 0 else dva[far]
        zz_out[i] = (mine + c_in[1, i].astype(F32)).astype(BF16)

    def q_step(n):
        r = n + 1 - 2 * (n % 2)
        unit = source(r)
        combine(unit)
        rdot = rdots[unit]
        dq_t = jnp.zeros((HD, UNIT), F32)
        for t in range(NT):
            rows = pl.ds(t * KT, KT)
            p = e_buf[unit, rows] * mst[unit, t // 4, t % 4 : t % 4 + 1]
            ds = p * (dp_buf[unit, rows] - rdot)
            dp_buf[unit, rows] = ds
            dq_t += dot(k_t[t // 4, :, t % 4 * KT : (t % 4 + 1) * KT], ds.astype(BF16))
        dq_acc[unit] = dq_t.T * SCALE
        scatter(r)

    def kv_step(unit, half, key=True, value=True):
        qu, dou, factor = q_s[unit], do_s[unit], mst[unit, half]
        for t in range(NT // 2):
            rows = pl.ds(half * 2 * SPAN + t * KT, KT)
            if value:
                dva[rows] += dot((e_buf[unit, rows] * factor[t : t + 1]).astype(BF16), dou)
            if key:
                dka[rows] += dot(dp_buf[unit, rows].astype(BF16), qu)

    repeat(0, 2, q_step)
    repeat(0, 2, lambda n: kv_step(source(n), 1))
    repeat(2, 4, q_step)
    repeat(2, 4, lambda n: kv_step(source(n), 1, key=False))
    c_start(1, 1)
    repeat(2, 4, lambda n: kv_step(source(n), 1, value=False))
    c_start(1, 0)
    deliver(1)
    deliver(0)
    zz_make(1)
    zz_copy[1].start()

    def near_step(n):
        kv_step(source(n), 0)

        @pl.when(n == 0)
        def _():
            zz_make(0)
            deliver(3)

        @pl.when(n == 2)
        def _():
            deliver(2)
            zz_copy[0].start()

    repeat(0, 4, near_step)
    c_start(0, 0)
    c_start(0, 1)

    for i in range(2):
        c_copy[0][i].wait_recv()
    near = pl.ds(0, SPAN)
    dka[near] = dka[near] * SCALE + c_in[0, 0].astype(F32)
    dva[near] = dva[near] + c_in[0, 1].astype(F32)
    stores = []
    for i, (near_sum, out) in enumerate(((dka, dk_hbm), (dva, dv_hbm))):
        zz_copy[i].wait_recv()
        done[i] = (near_sum[near] + zz_in[i].astype(F32)).astype(BF16)
        stores.append(pltpu.make_async_copy(done.at[i], out, loc_sem.at[1 + i]))
        stores[i].start()

    for r in range(4):
        f_part(r).wait_recv()

    keep.wait()
    for store in stores:
        store.wait()
    drain_a()
    for n in range(2):
        for i in range(2):
            c_copy[n][i].wait_send()
    for i in range(2):
        zz_copy[i].wait_send()
    for r in range(4):
        r_three(r).wait_send()
        f_part(r).wait_send()


def assemble(f_ref, dk_in, dv_in, dq_ref, dk_ref, dv_ref):
    out = []
    for b in range(KH):
        first = (b % 2) * 8 + b // 2
        blk = f_ref[first].astype(F32) + f_ref[first + 4].astype(F32)
        out += [blk[a * OWN : (a + 1) * OWN] for a in range(SHARE)]
    dq_ref[...] = jnp.concatenate(out, axis=1).astype(BF16)
    dk_ref[...] = dk_in[...]
    dv_ref[...] = dv_in[...]


def on_device(queries, grad_out, keys, values, prompt_len, resp_len):
    vmem = pl.BlockSpec(memory_space=pltpu.VMEM)
    smem = pl.BlockSpec(memory_space=pltpu.SMEM)
    hbm = pl.BlockSpec(memory_space=pl.ANY)
    dma = pltpu.SemaphoreType.DMA
    parts = pl.pallas_call(
        kernel,
        out_shape=[
            jax.ShapeDtypeStruct((16, BLK + 8, HD), BF16),
            jax.ShapeDtypeStruct((SPAN, HD), BF16),
            jax.ShapeDtypeStruct((SPAN, HD), BF16),
        ],
        in_specs=[smem, smem, hbm, hbm, hbm, hbm],
        out_specs=[hbm, hbm, hbm],
        scratch_shapes=[
            pltpu.VMEM((OWN, QH * HD), BF16),
            pltpu.VMEM((OWN, QH * HD), BF16),
            pltpu.VMEM((2, 4, 2 * BLK, HD), BF16),
            pltpu.VMEM((4, 4, 2 * BLK, HD), BF16),
            pltpu.VMEM((4, 16, 2 * BLK, HD), BF16),
            pltpu.VMEM((4, UNIT, HD), BF16),
            pltpu.VMEM((4, UNIT, HD), BF16),
            pltpu.VMEM((4, 2, SPAN, HD), BF16),
            pltpu.VMEM((2, HD, 2 * SPAN), BF16),
            pltpu.VMEM((4, KEYS, UNIT), F32),
            pltpu.VMEM((4, KEYS, UNIT), F32),
            pltpu.VMEM((4, 2, NT // 2, UNIT), F32),
            pltpu.VMEM((4, 8, UNIT), F32),
            pltpu.VMEM((4, 8, 16, HD), F32),
            pltpu.VMEM((4, 1, UNIT), F32),
            pltpu.VMEM((KEYS, HD), F32),
            pltpu.VMEM((KEYS, HD), F32),
            pltpu.VMEM((4, UNIT, HD), F32),
            pltpu.VMEM((4, 4, 4 * BLK, HD), BF16),
            pltpu.VMEM((4, 4, 4 * BLK, HD), BF16),
            pltpu.VMEM((4, 4, BLK + 8, HD), BF16),
            pltpu.VMEM((2, 2, SPAN, HD), BF16),
            pltpu.VMEM((2, 2, SPAN, HD), BF16),
            pltpu.VMEM((2, SPAN, HD), BF16),
            pltpu.VMEM((2, SPAN, HD), BF16),
            pltpu.VMEM((2, SPAN, HD), BF16),
            dma((4,)),
            dma((4, 2)),
            dma((4, 2)),
            dma((4, 4)),
            dma((4, 4)),
            dma((4,)),
            dma((4,)),
            dma((4,)),
            dma((4,)),
            dma((4,)),
            dma((4,)),
            dma((4,)),
            dma((4,)),
            dma((2, 2, 2)),
            dma((2, 2)),
        ],
        compiler_params=pltpu.CompilerParams(
            collective_id=0, has_side_effects=True, vmem_limit_bytes=60 * 2**20
        ),
        name="window_grads",
    )(prompt_len, resp_len, queries, grad_out, keys, values)
    return pl.pallas_call(
        assemble,
        out_shape=[
            jax.ShapeDtypeStruct((OWN, QH * HD), BF16),
            jax.ShapeDtypeStruct((SPAN, HD), BF16),
            jax.ShapeDtypeStruct((SPAN, HD), BF16),
        ],
        in_specs=[vmem] * 3,
        out_specs=[vmem] * 3,
        name="assemble",
    )(*parts)


def solution(mesh):
    in_specs = (
        P(("group", "ctx"), None),
        P(("group", "ctx"), None),
        P("ctx", None),
        P("ctx", None),
        P(),
        P("group", None),
    )
    out_specs = (P(("group", "ctx"), None), P("ctx", "group"), P("ctx", "group"))
    return jax.shard_map(
        on_device, mesh=mesh, in_specs=in_specs, out_specs=out_specs, check_vma=False
    )
```
